256 devices in a mesh: chan: 128 (over x, z, y), radial: 2 (over core).
Axes of the slice: x: 4, y: 4, z: 8, core: 2. Of those that a mesh axis runs over, the one named last changes fastest.
Arguments:
- wave: bfloat16 [512, 2, 6, 256, 384], P('chan', None, None, 'radial'), may hold values from -6 to 6
- l_values: int32 [512, 3], P('chan'), may hold values from 0 to 3
- couple_source: int32 [512, 8], replicated, may hold values from 0 to 511, as said below
- couple_pair: int32 [512, 8], P('chan'), may hold values from 0 to 2
- couple_order: int32 [512, 8], P('chan'), may hold values from 0 to 3
- couple_weight: float32 [512, 8], P('chan'), may hold values from -4 to 4
- channel_slot: int32 [512], replicated, may hold values from 0 to 511, as said below
Outputs:
- diag_step: bfloat16 [512, 2, 4, 256, 384], P('chan', None, None, 'radial')
- coupling_rate: bfloat16 [512, 2, 4, 256, 384], P('chan', None, None, 'radial')
The draws below stay inside these ranges and needn't reach their ends.
Inputs may be any that keep to these rules, and one draw needn't show every extreme that they name: `couple_source`: with slot = channel_slot of an entry's source and the entry's own slot, slot // 4 of the two differ by at most 2; the entries of the 4 channels in the slots of one device name at most 2 distinct source channels whose slots lie on any one other device, and exactly 2 for some device and every offset up to 2. Each channel has 8 entries. `channel_slot`: A permutation: the slot of each channel.
All inputs are finite; a program needn't handle non-finite values.
Results may differ from the reference program's by a relative error of at most 0.001.
Values may be sent and summed in bfloat16 or wider, within the bound.
No kernel may reach another device: no remote copies, remote signals or barrier semaphores. Data moves between devices by JAX's collectives and lax.ppermute only.
A program may use at most 192 MiB of HBM per device.

```python
import jax
import jax.numpy as jnp
from jax import lax

CH_DEV = 4
CHANNELS = 512
R1 = 256
R2 = 384
PLANES = 4
WSTART = 16
NPART = 8
BAND = 2
CAP = 2
KMAX = 4


def coupling_layout(key):
    device_count = CHANNELS // CH_DEV
    key_list = jax.random.split(key, 4)
    slot_channel = jax.random.permutation(key_list[0], CHANNELS).astype(jnp.int32)
    slot_map = jnp.zeros((CHANNELS,), jnp.int32).at[slot_channel].set(jnp.arange(CHANNELS, dtype=jnp.int32))
    starts = jax.random.randint(key_list[1], (device_count, 2 * BAND + 1), 0, CH_DEV)
    offset_draw = jax.random.randint(key_list[2], (CHANNELS, NPART), 0, 2 * (2 * BAND + 1))
    candidate = jax.random.randint(key_list[3], (CHANNELS, NPART), 0, CAP)
    slot_index = jnp.arange(CHANNELS, dtype=jnp.int32)[:, None]
    device = slot_index // CH_DEV
    target = slot_index % CH_DEV
    entry_index = jnp.arange(NPART, dtype=jnp.int32)[None, :]
    offset = jnp.where(offset_draw < 2 * BAND + 1, offset_draw - BAND, 0)
    forced = (device == device_count // 2) & (target < CAP) & (entry_index < 2 * BAND + 1)
    offset = jnp.where(forced, entry_index - BAND, offset)
    candidate = jnp.where(forced, target, candidate)
    source_device = device + offset
    outside = (source_device < 0) | (source_device >= device_count)
    source_device = jnp.where(outside, device - offset, source_device)
    actual = source_device - device + BAND
    start_here = starts[jnp.broadcast_to(device, (CHANNELS, NPART)), actual]
    local_index = (start_here + candidate) % CH_DEV
    source = slot_channel[source_device * CH_DEV + local_index]
    return (source.astype(jnp.int32), slot_map)


def draw_couple_source(key, part):
    source, slot_map = coupling_layout(key)
    return source


def draw_channel_slot(key, part):
    source, slot_map = coupling_layout(key)
    return slot_map


def set_ends(entries, rng, smallest, largest):
    longest = entries.shape.index(max(entries.shape))
    spots = []
    for shift in (0, 1):
        where = [jax.random.randint(jax.random.fold_in(rng, axis), (), 0, length) for axis, length in enumerate(entries.shape)]
        where[longest] = (where[longest] + shift) % entries.shape[longest]
        spots.append(tuple(where))
    return entries.at[spots[0]].set(smallest).at[spots[1]].set(largest)


def block_scale(key, dims, shards, low, top_value):
    def one(axis_at, parts):
        draws = jax.random.uniform(jax.random.fold_in(jax.random.fold_in(key, 6), axis_at), (parts,), jnp.float32, low / len(shards), top_value / len(shards))
        return jnp.repeat(jnp.exp(draws), dims[axis_at] // parts).reshape((-1,) + (1,) * (len(dims) - axis_at - 1))

    gain = one(*shards[0])
    for cut in shards[1:]:
        gain = gain * one(*cut)
    return gain


def gaussian(key, dims, scale, reach, pieces=(), held_as=jnp.bfloat16):
    array = jax.random.normal(key, dims, jnp.float32) * scale
    if len(pieces) > 0:
        array = block_scale(key, dims, pieces, -0.22, 0.18) * array
    return jnp.clip(array, min=-reach, max=reach).astype(held_as)


def setup_inputs(seed: int = 0) -> dict:
    streams_of = jax.random.split(jax.random.key(seed), 8)
    return {
        "wave": gaussian(streams_of[0], (CHANNELS, 2, PLANES + 2, R1, R2), 1.0, 6.0, ((0, 128), (3, 2))),
        "l_values": set_ends(jax.random.randint(streams_of[1], (CHANNELS, 3), 0, 4), jax.random.fold_in(streams_of[1], 1), 0, 3).astype(jnp.int32),
        "couple_source": draw_couple_source(jax.random.fold_in(streams_of[7], 71), 0),
        "couple_pair": set_ends(jax.random.randint(streams_of[3], (CHANNELS, NPART), 0, 3), jax.random.fold_in(streams_of[3], 1), 0, 2).astype(jnp.int32),
        "couple_order": set_ends(jax.random.randint(streams_of[4], (CHANNELS, NPART), 0, KMAX), jax.random.fold_in(streams_of[4], 1), 0, KMAX - 1).astype(jnp.int32),
        "couple_weight": gaussian(streams_of[5], (CHANNELS, NPART), 1.0, 4.0, ((0, 128),), jnp.float32),
        "channel_slot": draw_channel_slot(jax.random.fold_in(streams_of[7], 71), 0),
    }


grid_step = 0.25
charge = 3.0
time_step = 0.02


def radii_of(anchor, number):
    return (anchor + jnp.arange(number, dtype=jnp.float32) + 1.0) * grid_step


def multipole(pair_kind, order_kind, r_one, r_two, r_three):
    first_radius = jnp.where(pair_kind == 2, r_two, r_one)
    second_radius = jnp.where(pair_kind == 0, r_two, r_three)
    lesser = jnp.minimum(first_radius, second_radius)
    greater = jnp.maximum(first_radius, second_radius)
    return (lesser / greater) ** order_kind.astype(jnp.float32) / greater


def potential(l_first, l_second, l_third, r_one, r_two, r_three):
    result = l_first * (l_first + 1.0) / (2.0 * r_one * r_one) - charge / r_one
    result = result + l_second * (l_second + 1.0) / (2.0 * r_two * r_two) - charge / r_two
    result = result + l_third * (l_third + 1.0) / (2.0 * r_three * r_three) - charge / r_three
    return result


def reference(wave, l_values, couple_source, couple_pair, couple_order, couple_weight, channel_slot):
    r_one = radii_of(0.0, R1)[None, :, None]
    r_two = radii_of(0.0, R2)[None, None, :]
    r_three = radii_of(float(WSTART), PLANES)[:, None, None]
    source_slot = channel_slot[couple_source]

    def one_channel(slot_index):
        upper_plane = wave[slot_index, :, 2:].astype(jnp.float32)
        lower_plane = wave[slot_index, :, :-2].astype(jnp.float32)
        centre = wave[slot_index, :, 1:-1].astype(jnp.float32)
        padded = jnp.pad(centre, ((0, 0), (0, 0), (1, 1), (1, 1)))
        across = padded[:, :, 2:, 1:-1] + padded[:, :, :-2, 1:-1] - 2.0 * centre
        along_two = padded[:, :, 1:-1, 2:] + padded[:, :, 1:-1, :-2] - 2.0 * centre
        planar = upper_plane + lower_plane - 2.0 * centre
        angular = l_values[slot_index].astype(jnp.float32)
        potential_field = potential(angular[0], angular[1], angular[2], r_one, r_two, r_three)
        energy = -0.5 * (across + along_two + planar) / (grid_step * grid_step) + potential_field * centre
        diagonal = jnp.stack([time_step * energy[1], -time_step * energy[0]]).astype(jnp.bfloat16)
        coupled_sum = jnp.zeros(centre.shape, jnp.float32)
        for entry_index in range(NPART):
            source = wave[source_slot[slot_index, entry_index], :, 1:-1].astype(jnp.float32)
            factor = couple_weight[slot_index, entry_index] * multipole(
                couple_pair[slot_index, entry_index], couple_order[slot_index, entry_index], r_one, r_two, r_three)
            coupled_sum = coupled_sum + factor * source
        coupled = jnp.stack([coupled_sum[1], -coupled_sum[0]]).astype(jnp.bfloat16)
        return diagonal, coupled

    diag_step, coupling_rate = lax.map(one_channel, jnp.arange(CHANNELS, dtype=jnp.int32))
    return diag_step, coupling_rate
```

```python
import functools

import jax
import jax.numpy as jnp
from jax import lax
from jax.experimental import pallas as pl
from jax.experimental.pallas import tpu as pltpu
from jax.sharding import PartitionSpec as P

WSTART = 16
grid_step = 0.25
charge = 3.0
time_step = 0.02

HELD = 4
PARTS = 8
PLANES = 4
ORDERS = 4
LISTED = 3
ENTRIES = HELD * PARTS
GROUPS = 7

PAIR_LOW = 1233667140
PAIR_HIGH = 1234062796


def two_of(mask):
    word = jnp.where(mask >= 8, PAIR_HIGH, PAIR_LOW)
    code = lax.shift_right_logical(word, 4 * (mask & 7)) & 15
    return code & 3, code >> 2


def needed(source_ref, slot_ref, device, offset, devices):
    reader = device + offset
    inside = (reader >= 0) & (reader < devices)
    row = jnp.clip(reader, 0, devices - 1) * HELD
    mask = jnp.int32(0)
    for i in range(HELD):
        for e in range(PARTS):
            slot = slot_ref[source_ref[e, row + i]]
            mask = mask | jnp.where(slot // HELD == device, jnp.int32(1) << (slot % HELD), 0)
    return two_of(jnp.where(inside, mask, 0))


def listed(first, second, pair):
    l1 = jnp.where(second != first, second, jnp.where(pair[0] != first, pair[0], pair[1]))
    l2 = jnp.where((pair[0] == first) | (pair[0] == l1), pair[1], pair[0])
    return first, l1, l2


def plan(source_ref, slot_ref, device, devices):
    near_up = needed(source_ref, slot_ref, device, 1, devices)
    near_down = needed(source_ref, slot_ref, device, -1, devices)
    far_up = needed(source_ref, slot_ref, device, 2, devices)
    far_down = needed(source_ref, slot_ref, device, -2, devices)

    def outside(value, pair):
        return (value != pair[0]) & (value != pair[1])

    best = None
    for a in (1, 0):
        for c in (1, 0):
            a_up, a_down = far_up[a], far_up[1 - a]
            c_up, c_down = far_down[c], far_down[1 - c]
            bad = (a_up != c_up) & outside(a_up, near_up) & outside(c_up, near_up)
            bad = bad | ((a_down != c_down) & outside(a_down, near_down) & outside(c_down, near_down))
            here = (a_up, a_down, c_up, c_down)
            if best is None:
                best = here
            else:
                best = tuple(jnp.where(bad, old, new) for old, new in zip(best, here))
    a_up, a_down, c_up, c_down = best
    up = listed(a_up, c_up, near_up)
    down = listed(c_down, a_down, near_down)
    return up, down, best


def run(copies):
    for copy in copies:
        copy.start()
    for copy in copies:
        copy.wait()


def gather(wave_ref, picks_ref, out_refs, sem, planes):
    copies = []
    for plane, (up_ref, down_ref) in zip(planes, out_refs):
        for i in range(LISTED):
            for base, ref in ((0, up_ref), (LISTED, down_ref)):
                copies.append(
                    pltpu.make_async_copy(
                        wave_ref.at[picks_ref[base + i], :, 1 + plane],
                        ref.at[i],
                        sem.at[len(copies)],
                    )
                )
    run(copies)


def first_kernel(
    devices, planes, me_ref, sources, slots, wave_ref, picks_ref, up_ref, down_ref, source_ref, slot_ref, sem
):
    run([
        pltpu.make_async_copy(sources, source_ref, sem.at[0]),
        pltpu.make_async_copy(slots, slot_ref, sem.at[1]),
    ])
    up, down, _ = plan(source_ref, slot_ref, me_ref[0], devices)
    for i in range(LISTED):
        picks_ref[i] = up[i]
        picks_ref[LISTED + i] = down[i]
    gather(wave_ref, picks_ref, [(up_ref, down_ref)], sem, planes)


def rest_kernel(planes, picks_ref, wave_ref, *refs):
    outs, sem = refs[:-1], refs[-1]
    gather(wave_ref, picks_ref, list(zip(outs[0::2], outs[1::2])), sem, planes)


def item_kernel(
    devices, me_ref, sources, slots, pair_ref, order_ref, count_ref, item_ref, pass_ref, source_ref, slot_ref, sem
):
    run([
        pltpu.make_async_copy(sources, source_ref, sem.at[0]),
        pltpu.make_async_copy(slots, slot_ref, sem.at[1]),
    ])
    me = me_ref[0]
    before = lax.rem(me + devices - 1, devices)
    after = lax.rem(me + 1, devices)
    up_before, _, far_before = plan(source_ref, slot_ref, before, devices)
    _, down_after, far_after = plan(source_ref, slot_ref, after, devices)
    pass_ref[0] = jnp.where(far_before[2] == far_before[0], 0, 1)
    pass_ref[1] = jnp.where(far_after[1] == far_after[3], 0, 1)
    _, _, far_two_before = plan(source_ref, slot_ref, lax.rem(me + devices - 2, devices), devices)
    _, _, far_two_after = plan(source_ref, slot_ref, lax.rem(me + 2, devices), devices)

    def among(value, three):
        return jnp.where(value == three[0], 0, jnp.where(value == three[1], 1, 2))

    for g in range(GROUPS):
        count_ref[g] = jnp.int32(0)
    for s in range(HELD):
        for e in range(PARTS):
            slot = slot_ref[source_ref[e, me * HELD + s]]
            local, offset = slot % HELD, slot // HELD - me
            group = jnp.where(offset == -1, 1, jnp.where(offset == 1, 2, 0))
            group = jnp.where(offset == -2, jnp.where(local == far_two_before[0], 3, 4), group)
            group = jnp.where(offset == 2, jnp.where(local == far_two_after[3], 5, 6), group)
            place = jnp.where(group == 0, local, 0)
            place = jnp.where(group == 1, among(local, up_before), place)
            place = jnp.where(group == 2, among(local, down_after), place)
            field = pair_ref[s, e] * ORDERS + order_ref[s, e]
            number = count_ref[group]
            item_ref[group, number] = (s * PARTS + e) + ENTRIES * (place + HELD * field)
            count_ref[group] = number + 1


def pass_kernel(pass_ref, up_ref, down_ref, up_one, down_one, down_three, up_three):
    up_one[...] = up_ref[0]
    down_one[...] = down_ref[0]
    down_three[...] = up_ref[pass_ref[0]]
    up_three[...] = down_ref[pass_ref[1]]


def radius(shape, dim, start):
    return (start + lax.broadcasted_iota(jnp.int32, shape, dim) + 1).astype(jnp.float32) * grid_step


def field_kernel(row_ref, *out_refs):
    shape = out_refs[0].shape[1:]
    step = 16

    def tile(i, carry):
        at = pl.ds(pl.multiple_of(i * step, step), step)
        part = (step, shape[1])
        r_one = radius(part, 0, row_ref[0] + i * step)
        r_two = radius(part, 1, 0)

        def write(refs, pair, left, right):
            greater = jnp.maximum(left, right)
            value = 1.0 / greater
            ratio = jnp.minimum(left, right) / greater
            for order in range(ORDERS):
                for ref in refs:
                    ref[pair * ORDERS + order, at] = jnp.broadcast_to(value, part)
                value = value * ratio

        write(out_refs, 0, r_one, r_two)
        for p, ref in enumerate(out_refs):
            r_three = (WSTART + p + 1) * grid_step
            write([ref], 1, r_one, r_three)
            write([ref], 2, r_two, r_three)
        return carry

    lax.fori_loop(0, shape[0] // step, tile, 0)


def diagonal_kernel(row_ref, l_ref, wave_ref, edge_ref, out_ref):
    s, c = pl.program_id(0), pl.program_id(1)
    rows, columns = wave_ref.shape[3:]
    shape = (rows, columns)
    r_one = radius((rows, 1), 0, row_ref[0])
    r_two = radius((1, columns), 1, 0)

    def centrifugal(electron):
        number = l_ref[s, electron].astype(jnp.float32)
        return number * (number + 1.0)

    first = centrifugal(0) / (2.0 * r_one * r_one) - charge / r_one
    second = centrifugal(1) / (2.0 * r_two * r_two) - charge / r_two
    sign = jnp.where(c == 1, time_step, -time_step)
    lower_half = row_ref[0] == 0
    row = lax.broadcasted_iota(jnp.int32, shape, 0)
    column = lax.broadcasted_iota(jnp.int32, shape, 1)
    for p in range(PLANES):
        r_three = (WSTART + p + 1) * grid_step
        third = centrifugal(2) / (2.0 * r_three * r_three) - charge / r_three
        centre = wave_ref[0, 0, p + 1].astype(jnp.float32)
        edge = edge_ref[0, 0, p : p + 1].astype(jnp.float32)
        above = jnp.where(lower_half, 0.0, edge)
        below = jnp.where(lower_half, edge, 0.0)
        total = wave_ref[0, 0, p].astype(jnp.float32) + wave_ref[0, 0, p + 2].astype(jnp.float32)
        total = total + jnp.where(row == 0, above, pltpu.roll(centre, 1, 0))
        total = total + jnp.where(row == rows - 1, below, pltpu.roll(centre, rows - 1, 0))
        total = total + jnp.where(column == 0, 0.0, pltpu.roll(centre, 1, 1))
        total = total + jnp.where(column == columns - 1, 0.0, pltpu.roll(centre, columns - 1, 1))
        potential = first + (second + (third + 3.0 / (grid_step * grid_step)))
        energy = potential * centre - (0.5 / (grid_step * grid_step)) * total
        out_ref[0, 0, p] = (sign * energy).astype(out_ref.dtype)


def add_items(group, count_ref, item_ref, weight_ref, field_ref, source_ref, total):
    rows = total.shape[2]
    step = 16

    def one(n, carry):
        code = item_ref[group, n]
        entry, rest = code % ENTRIES, code // ENTRIES
        s, e = entry // PARTS, entry % PARTS
        place, field = rest % HELD, rest // HELD
        weight = weight_ref[s, e]
        for i in range(rows // step):
            at = pl.ds(i * step, step)
            factor = weight * field_ref[field, at]
            for c in range(2):
                total[s, c, at] += factor * source_ref[place, c, at].astype(jnp.float32)
        return carry

    lax.fori_loop(0, count_ref[group], one, 0)


def near_kernel(
    plane, count_ref, item_ref, weight_ref, wave_ref, up_ref, down_ref, field_ref, total, own, sem
):
    copy = pltpu.make_async_copy(wave_ref.at[:, :, 1 + plane], own, sem)
    copy.start()
    total[...] = jnp.zeros_like(total)
    copy.wait()
    for group, ref in ((0, own), (1, up_ref), (2, down_ref)):
        add_items(group, count_ref, item_ref, weight_ref, field_ref, ref, total)


def far_kernel(plane, count_ref, item_ref, weight_ref, near, *refs):
    far_refs, field_ref = refs[:4], refs[4]
    out_ref, total, staged, sem = refs[-4:]
    total[...] = near[...]
    for i, ref in enumerate(far_refs):
        add_items(3 + i, count_ref, item_ref, weight_ref, field_ref, ref, total)
    copies = []
    for s in range(HELD):
        staged[s, 0] = total[s, 1].astype(staged.dtype)
        staged[s, 1] = (-total[s, 0]).astype(staged.dtype)
        copies.append(pltpu.make_async_copy(staged.at[s], out_ref.at[s, :, plane], sem.at[s]))
        copies[-1].start()
    for copy in copies:
        copy.wait()


ANY = pl.BlockSpec(memory_space=pl.ANY)
HBM = pl.BlockSpec(memory_space=pltpu.HBM)
VMEM = pl.BlockSpec(memory_space=pltpu.VMEM)
SMEM = pl.BlockSpec(memory_space=pltpu.SMEM)


def params(mib):
    return pltpu.CompilerParams(vmem_limit_bytes=mib << 20)


def cost(micros):
    return pl.CostEstimate(flops=0, bytes_accessed=micros * 3_000_000, transcendentals=0)


def behind(value, *others):
    return lax.optimization_barrier((value, others))[0]


def shards(wave, l_values, couple_source, couple_pair, couple_order, couple_weight, channel_slot):
    devices = lax.axis_size("chan")
    rows, columns = wave.shape[3:]
    me = lax.axis_index("chan").astype(jnp.int32).reshape(1)
    core = lax.axis_index("radial").astype(jnp.int32)
    row_start = (core * rows).reshape(1)
    bf16 = wave.dtype
    message = jax.ShapeDtypeStruct((LISTED, 2, rows, columns), bf16)
    one = jax.ShapeDtypeStruct((2, rows, columns), bf16)
    total = jax.ShapeDtypeStruct((HELD, 2, rows, columns), jnp.float32)
    sources = couple_source.T
    index_scratch = [pltpu.SMEM(sources.shape, jnp.int32), pltpu.SMEM(channel_slot.shape, jnp.int32)]

    def dma(number):
        return pltpu.SemaphoreType.DMA((number,))

    def shift(array, by):
        return lax.ppermute(array, "chan", [(i, (i + by) % devices) for i in range(devices)])

    picks, up0, down0 = pl.pallas_call(
        functools.partial(first_kernel, devices, [0]),
        out_shape=(jax.ShapeDtypeStruct((2 * LISTED,), jnp.int32), message, message),
        in_specs=[SMEM, HBM, HBM, HBM],
        out_specs=(SMEM, VMEM, VMEM),
        scratch_shapes=[*index_scratch, dma(2 * LISTED)],
        compiler_params=params(8),
        cost_estimate=cost(3),
        name="first_kernel",
    )(me, sources, channel_slot, wave)
    later = list(range(1, PLANES))
    rest = pl.pallas_call(
        functools.partial(rest_kernel, later),
        out_shape=[message] * (2 * len(later)),
        in_specs=[SMEM, HBM],
        out_specs=[VMEM] * (2 * len(later)),
        scratch_shapes=[dma(2 * LISTED * len(later))],
        compiler_params=params(8),
        cost_estimate=cost(2),
        name="rest_kernel",
    )(picks, wave)
    ups = [shift(v, 1) for v in [up0] + list(rest[0::2])]
    downs = [shift(v, -1) for v in [down0] + list(rest[1::2])]

    wave_late, me_late, start_late = behind((wave, me, row_start), *rest)
    edge = jnp.where(core == 0, wave_late[:, :, 1:-1, rows - 1], wave_late[:, :, 1:-1, 0])
    edge = lax.ppermute(edge, "radial", [(0, 1), (1, 0)])

    count, item, passed = pl.pallas_call(
        functools.partial(item_kernel, devices),
        out_shape=(
            jax.ShapeDtypeStruct((GROUPS,), jnp.int32),
            jax.ShapeDtypeStruct((GROUPS, ENTRIES), jnp.int32),
            jax.ShapeDtypeStruct((2,), jnp.int32),
        ),
        in_specs=[SMEM, HBM, HBM, SMEM, SMEM],
        out_specs=(SMEM,) * 3,
        scratch_shapes=[*index_scratch, dma(2)],
        compiler_params=params(4),
        cost_estimate=cost(6),
        name="item_kernel",
    )(me_late, sources, channel_slot, couple_pair, couple_order)

    fields = pl.pallas_call(
        field_kernel,
        out_shape=[jax.ShapeDtypeStruct((3 * ORDERS, rows, columns), jnp.float32)] * PLANES,
        in_specs=[SMEM],
        out_specs=[VMEM] * PLANES,
        compiler_params=params(16),
        cost_estimate=cost(2),
        name="field_kernel",
    )(behind(start_late, count))

    diag_step = pl.pallas_call(
        diagonal_kernel,
        grid=(HELD, 2),
        out_shape=jax.ShapeDtypeStruct((HELD, 2, PLANES, rows, columns), bf16),
        in_specs=[
            SMEM,
            SMEM,
            pl.BlockSpec((1, 1, PLANES + 2, rows, columns), lambda s, c: (s, c, 0, 0, 0)),
            pl.BlockSpec((1, 1, PLANES, columns), lambda s, c: (s, c, 0, 0)),
        ],
        out_specs=pl.BlockSpec((1, 1, PLANES, rows, columns), lambda s, c: (s, 1 - c, 0, 0, 0)),
        compiler_params=params(10),
        cost_estimate=cost(7),
        name="diagonal_kernel",
    )(behind(start_late, fields), l_values, wave, edge)

    fars, nears = [], []
    last = diag_step
    for p in range(PLANES):
        up, down = behind((ups[p], downs[p]), last)
        up_one, down_one, down_three, up_three = pl.pallas_call(
            pass_kernel,
            out_shape=(one,) * 4,
            in_specs=[SMEM, VMEM, VMEM],
            out_specs=(VMEM,) * 4,
            compiler_params=params(8),
            cost_estimate=cost(1),
            name="pass_kernel",
        )(passed, up, down)
        fars.append([v[None] for v in (shift(up_one, 1), shift(up_three, 3), shift(down_one, -1), shift(down_three, -3))])
        weights = behind(couple_weight, up_one)
        near = pl.pallas_call(
            functools.partial(near_kernel, p),
            out_shape=total,
            in_specs=[SMEM] * 3 + [HBM] + [VMEM] * 3,
            out_specs=VMEM,
            scratch_shapes=[pltpu.VMEM((HELD, 2, rows, columns), bf16), pltpu.SemaphoreType.DMA(())],
            compiler_params=params(12),
            cost_estimate=cost(3),
            name="near_kernel",
        )(count, item, weights, wave, up, down, fields[p])
        nears.append(near)
        last = near

    coupling = None
    for p in range(PLANES):
        inputs = [count, item, couple_weight, nears[p], *fars[p], fields[p]]
        specs = [SMEM] * 3 + [VMEM] * 6
        if p == 0:
            inputs[0] = behind(count, last)
        aliases = {}
        if coupling is not None:
            aliases = {len(inputs): 0}
            inputs.append(coupling)
            specs.append(ANY)
        coupling = pl.pallas_call(
            functools.partial(far_kernel, p),
            out_shape=jax.ShapeDtypeStruct((HELD, 2, PLANES, rows, columns), bf16),
            in_specs=specs,
            out_specs=ANY,
            scratch_shapes=[
                pltpu.VMEM(total.shape, total.dtype),
                pltpu.VMEM((HELD, 2, rows, columns), bf16),
                dma(HELD),
            ],
            input_output_aliases=aliases,
            compiler_params=params(12),
            cost_estimate=cost(2),
            name="far_kernel",
        )(*inputs)
    return diag_step, coupling


def solution(mesh):
    placed = (
        P("chan", None, None, "radial", None),
        P("chan", None),
        P(),
        P("chan", None),
        P("chan", None),
        P("chan", None),
        P(),
    )
    return jax.shard_map(
        shards,
        mesh=mesh,
        in_specs=placed,
        out_specs=(P("chan", None, None, "radial", None), P("chan", None, None, "radial", None)),
        check_vma=False,
    )
```

```python
import functools

import jax
import jax.numpy as jnp
from jax import lax
from jax.experimental import pallas as pl
from jax.experimental.pallas import tpu as pltpu
from jax.sharding import PartitionSpec as P

WSTART = 16
grid_step = 0.25
charge = 3.0
time_step = 0.02

HELD = 4
PARTS = 8
PLANES = 4
HALF = 2
EDGE = 16
ORDERS = 4
ENTRIES = HELD * PARTS
GROUPS = 5

PAIR_LOW = 1233667140
PAIR_HIGH = 1234062796


def two_of(mask):
    word = jnp.where(mask >= 8, PAIR_HIGH, PAIR_LOW)
    code = lax.shift_right_logical(word, 4 * (mask & 7)) & 15
    return code & 3, code >> 2


def needed(source_ref, slot_ref, device, offset, devices):
    reader = device + offset
    inside = (reader >= 0) & (reader < devices)
    row = jnp.clip(reader, 0, devices - 1) * HELD
    mask = jnp.int32(0)
    for i in range(HELD):
        for e in range(PARTS):
            slot = slot_ref[source_ref[e, row + i]]
            mask = mask | jnp.where(slot // HELD == device, jnp.int32(1) << (slot % HELD), 0)
    return two_of(jnp.where(inside, mask, 0))


def run(copies):
    for copy in copies:
        copy.start()
    for copy in copies:
        copy.wait()


def head_kernel(wave_ref, up_ref, down_ref, up_held, down_held, in_sem, out_sem):
    steps = []
    for s in range(HELD):
        for ref, held, start in ((up_ref, up_held, 0), (down_ref, down_held, HALF)):
            n = len(steps)
            steps.append((
                pltpu.make_async_copy(wave_ref.at[s, :, pl.ds(1 + start, HALF)], held.at[s], in_sem.at[n]),
                pltpu.make_async_copy(held.at[s], ref.at[s], out_sem.at[n]),
            ))
    for come, _ in steps:
        come.start()
    for come, go in steps:
        come.wait()
        go.start()
    for _, go in steps:
        go.wait()


def select_kernel(
    devices,
    edge_rows,
    me_ref,
    core_ref,
    sources,
    slots,
    wave_ref,
    up_ref,
    down_ref,
    edge_ref,
    source_ref,
    slot_ref,
    sem,
):
    rows = wave_ref.shape[3]
    at = pl.multiple_of((1 - core_ref[0]) * (rows - edge_rows), edge_rows)
    edge = pltpu.make_async_copy(
        wave_ref.at[:, :, pl.ds(1, PLANES), pl.ds(at, edge_rows)], edge_ref, sem.at[0]
    )
    edge.start()
    run([
        pltpu.make_async_copy(sources, source_ref, sem.at[1]),
        pltpu.make_async_copy(slots, slot_ref, sem.at[2]),
    ])
    me = me_ref[0]
    copies = []
    for ref, offset, start in ((up_ref, 1, HALF), (down_ref, -1, 0)):
        for i, pick in enumerate(needed(source_ref, slot_ref, me, offset, devices)):
            copies.append(
                pltpu.make_async_copy(
                    wave_ref.at[pick, :, pl.ds(1 + start, HALF)], ref.at[i], sem.at[3 + len(copies)]
                )
            )
    run(copies)
    edge.wait()


def item_kernel(
    devices, me_ref, sources, slots, pair_ref, order_ref, count_ref, item_ref, pass_ref, source_ref, slot_ref, sem
):
    run([
        pltpu.make_async_copy(sources, source_ref, sem.at[0]),
        pltpu.make_async_copy(slots, slot_ref, sem.at[1]),
    ])
    me = me_ref[0]

    def other(by):
        return lax.rem(me + by + devices, devices)

    for i, (by, offset) in enumerate(((-1, 2), (-1, -2), (1, -2), (1, 2))):
        pair = needed(source_ref, slot_ref, other(by), offset, devices)
        pass_ref[2 * i] = pair[0]
        pass_ref[2 * i + 1] = pair[1]
    firsts = [needed(source_ref, slot_ref, other(by), -by, devices)[0] for by in (-1, 1, -2, 2)]
    for g in range(GROUPS):
        count_ref[g] = jnp.int32(0)
    for s in range(HELD):
        for e in range(PARTS):
            slot = slot_ref[source_ref[e, me * HELD + s]]
            local, offset = slot % HELD, slot // HELD - me
            group, first = jnp.int32(0), jnp.int32(0)
            for g, by in enumerate((-1, 1, -2, 2)):
                group = jnp.where(offset == by, g + 1, group)
                first = jnp.where(offset == by, firsts[g], first)
            place = jnp.where(local == first, 0, 1)
            field = pair_ref[s, e] * ORDERS + order_ref[s, e]
            number = count_ref[group]
            item_ref[group, number] = (s * PARTS + e) + ENTRIES * (local + HELD * (place + 2 * field))
            count_ref[group] = number + 1


def pass_kernel(first, pass_ref, all_ref, one_ref, three_ref):
    for i in range(2):
        one_ref[i] = all_ref[pass_ref[first + i]]
        three_ref[i] = all_ref[pass_ref[first + 2 + i]]


def radius(shape, dim, start):
    return (start + lax.broadcasted_iota(jnp.int32, shape, dim) + 1).astype(jnp.float32) * grid_step


def field_kernel(row_ref, *out_refs):
    shape = out_refs[0].shape[1:]
    step = 16

    def tile(i, carry):
        at = pl.ds(pl.multiple_of(i * step, step), step)
        part = (step, shape[1])
        r_one = radius(part, 0, row_ref[0] + i * step)
        r_two = radius(part, 1, 0)

        def write(refs, pair, left, right):
            greater = jnp.maximum(left, right)
            value = 1.0 / greater
            ratio = jnp.minimum(left, right) / greater
            for order in range(ORDERS):
                for ref in refs:
                    ref[pair * ORDERS + order, at] = jnp.broadcast_to(value, part)
                value = value * ratio

        write(out_refs, 0, r_one, r_two)
        for p, ref in enumerate(out_refs):
            r_three = (WSTART + p + 1) * grid_step
            write([ref], 1, r_one, r_three)
            write([ref], 2, r_two, r_three)
        return carry

    lax.fori_loop(0, shape[0] // step, tile, 0)


def diagonal_kernel(row_ref, l_ref, wave_ref, edge_ref, out_ref):
    s, c = pl.program_id(0), pl.program_id(1)
    rows, columns = wave_ref.shape[3:]
    shape = (rows, columns)
    r_one = radius((rows, 1), 0, row_ref[0])
    r_two = radius((1, columns), 1, 0)

    def centrifugal(electron):
        number = l_ref[s, electron].astype(jnp.float32)
        return number * (number + 1.0)

    first = centrifugal(0) / (2.0 * r_one * r_one) - charge / r_one
    second = centrifugal(1) / (2.0 * r_two * r_two) - charge / r_two
    sign = jnp.where(c == 1, time_step, -time_step)
    lower_half = row_ref[0] == 0
    row = lax.broadcasted_iota(jnp.int32, shape, 0)
    column = lax.broadcasted_iota(jnp.int32, shape, 1)
    for p in range(PLANES):
        r_three = (WSTART + p + 1) * grid_step
        third = centrifugal(2) / (2.0 * r_three * r_three) - charge / r_three
        centre = wave_ref[0, 0, p + 1].astype(jnp.float32)
        edge = edge_ref[0, 0, p].astype(jnp.float32)
        above = jnp.where(lower_half, 0.0, edge[-1:])
        below = jnp.where(lower_half, edge[:1], 0.0)
        total = wave_ref[0, 0, p].astype(jnp.float32) + wave_ref[0, 0, p + 2].astype(jnp.float32)
        total = total + jnp.where(row == 0, above, pltpu.roll(centre, 1, 0))
        total = total + jnp.where(row == rows - 1, below, pltpu.roll(centre, rows - 1, 0))
        total = total + jnp.where(column == 0, 0.0, pltpu.roll(centre, 1, 1))
        total = total + jnp.where(column == columns - 1, 0.0, pltpu.roll(centre, columns - 1, 1))
        potential = first + (second + (third + 3.0 / (grid_step * grid_step)))
        energy = potential * centre - (0.5 / (grid_step * grid_step)) * total
        out_ref[0, 0, p] = (sign * energy).astype(out_ref.dtype)


def add_items(group, selected, p, count_ref, item_ref, weight_ref, field_ref, source_ref, total):
    rows = total.shape[2]
    step = 16

    def one(n, carry):
        code = item_ref[group, n]
        entry, rest = code % ENTRIES, code // ENTRIES
        s, e = entry // PARTS, entry % PARTS
        local, rest = rest % HELD, rest // HELD
        place, field = rest % 2, rest // 2
        place = place if selected else local
        weight = weight_ref[s, e]
        for i in range(rows // step):
            at = pl.ds(i * step, step)
            factor = weight * field_ref[field, at]
            for c in range(2):
                total[s, c, at] += factor * source_ref[place, c, p, at].astype(jnp.float32)
        return carry

    lax.fori_loop(0, count_ref[group], one, 0)


def own_kernel(count_ref, item_ref, weight_ref, wave_ref, up_all, down_all, *refs):
    fields, totals, own, sem = refs[:PLANES], refs[PLANES : 2 * PLANES], refs[-2], refs[-1]
    copy = pltpu.make_async_copy(wave_ref.at[:, :, pl.ds(1, PLANES)], own, sem)
    copy.start()
    for total in totals:
        total[...] = jnp.zeros_like(total)
    copy.wait()
    for p in range(PLANES):
        common = count_ref, item_ref, weight_ref, fields[p]
        add_items(0, False, p, *common, own, totals[p])
        group, ref = (1, up_all) if p < HALF else (2, down_all)
        add_items(group, False, p % HALF, *common, ref, totals[p])


def near_kernel(count_ref, item_ref, weight_ref, up_two, down_two, *refs):
    fields, totals = refs[:PLANES], refs[-PLANES:]
    for p in range(PLANES):
        group, ref = (2, down_two) if p < HALF else (1, up_two)
        add_items(group, True, p % HALF, count_ref, item_ref, weight_ref, fields[p], ref, totals[p])


def last_kernel(count_ref, item_ref, weight_ref, up_one, down_three, down_one, up_three, *refs):
    fields, totals = refs[:PLANES], refs[-2 - PLANES : -2]
    out_ref, (staged, sem) = refs[-3 - PLANES], refs[-2:]
    copies = []
    for p, total in enumerate(totals):
        common = count_ref, item_ref, weight_ref, fields[p]
        for group, ref in ((3, up_one), (4, down_three)) if p < HALF else ((4, down_one), (3, up_three)):
            add_items(group, True, p % HALF, *common, ref, total)
        for s in range(HELD):
            staged[p, s, 0] = total[s, 1].astype(staged.dtype)
            staged[p, s, 1] = (-total[s, 0]).astype(staged.dtype)
            copies.append(
                pltpu.make_async_copy(staged.at[p, s], out_ref.at[s, :, p], sem.at[p * HELD + s])
            )
            copies[-1].start()
    for copy in copies:
        copy.wait()


ANY = pl.BlockSpec(memory_space=pl.ANY)
HBM = pl.BlockSpec(memory_space=pltpu.HBM)
VMEM = pl.BlockSpec(memory_space=pltpu.VMEM)
SMEM = pl.BlockSpec(memory_space=pltpu.SMEM)


def params(mib):
    return pltpu.CompilerParams(vmem_limit_bytes=mib << 20)


def cost(micros):
    return pl.CostEstimate(flops=0, bytes_accessed=micros * 3_000_000, transcendentals=0)


def behind(value, *others):
    return lax.optimization_barrier((value, others))[0]


def shards(wave, l_values, couple_source, couple_pair, couple_order, couple_weight, channel_slot):
    devices = lax.axis_size("chan")
    rows, columns = wave.shape[3:]
    me = lax.axis_index("chan").astype(jnp.int32).reshape(1)
    core = lax.axis_index("radial").astype(jnp.int32)
    row_start = (core * rows).reshape(1)
    bf16 = wave.dtype

    def array(*lead, dtype=bf16):
        return jax.ShapeDtypeStruct((*lead, rows, columns), dtype)

    sources = couple_source.T
    index_scratch = [pltpu.SMEM(sources.shape, jnp.int32), pltpu.SMEM(channel_slot.shape, jnp.int32)]

    def dma(number):
        return pltpu.SemaphoreType.DMA((number,))

    def shift(array, by):
        return lax.ppermute(array, "chan", [(i, (i + by) % devices) for i in range(devices)])

    up_all, down_all = pl.pallas_call(
        head_kernel,
        out_shape=[array(HELD, 2, HALF)] * 2,
        in_specs=[HBM],
        out_specs=[ANY] * 2,
        scratch_shapes=[pltpu.VMEM((HELD, 2, HALF, rows, columns), bf16)] * 2 + [dma(2 * HELD)] * 2,
        compiler_params=params(60),
        cost_estimate=cost(2),
        name="head_kernel",
    )(wave)
    wave = behind(wave, up_all)
    up_all, down_all = shift(up_all, 1), shift(down_all, -1)
    up_two, down_two, edge = pl.pallas_call(
        functools.partial(select_kernel, devices, EDGE),
        out_shape=[*[array(2, 2, HALF)] * 2, jax.ShapeDtypeStruct((HELD, 2, PLANES, EDGE, columns), bf16)],
        in_specs=[SMEM, SMEM, HBM, HBM, HBM],
        out_specs=[VMEM] * 3,
        scratch_shapes=[*index_scratch, dma(7)],
        compiler_params=params(60),
        cost_estimate=cost(3),
        name="select_kernel",
    )(me, core.reshape(1), sources, channel_slot, wave)
    me_late, start_late = behind((me, row_start), up_two)
    up_two = shift(up_two, 1)
    down_two = shift(down_two, -1)
    edge = lax.ppermute(edge, "radial", [(0, 1), (1, 0)])

    count, item, passed = pl.pallas_call(
        functools.partial(item_kernel, devices),
        out_shape=(
            jax.ShapeDtypeStruct((GROUPS,), jnp.int32),
            jax.ShapeDtypeStruct((GROUPS, ENTRIES), jnp.int32),
            jax.ShapeDtypeStruct((8,), jnp.int32),
        ),
        in_specs=[SMEM, HBM, HBM, SMEM, SMEM],
        out_specs=(SMEM,) * 3,
        scratch_shapes=[*index_scratch, dma(2)],
        compiler_params=params(4),
        cost_estimate=cost(6),
        name="item_kernel",
    )(me_late, sources, channel_slot, couple_pair, couple_order)

    fields = pl.pallas_call(
        field_kernel,
        out_shape=[array(3 * ORDERS, dtype=jnp.float32)] * PLANES,
        in_specs=[SMEM],
        out_specs=[VMEM] * PLANES,
        compiler_params=params(16),
        cost_estimate=cost(2),
        name="field_kernel",
    )(behind(start_late, count))

    diag_step = pl.pallas_call(
        diagonal_kernel,
        grid=(HELD, 2),
        out_shape=array(HELD, 2, PLANES),
        in_specs=[
            SMEM,
            SMEM,
            pl.BlockSpec((1, 1, PLANES + 2, rows, columns), lambda s, c: (s, c, 0, 0, 0)),
            pl.BlockSpec((1, 1, PLANES, EDGE, columns), lambda s, c: (s, c, 0, 0, 0)),
        ],
        out_specs=pl.BlockSpec((1, 1, PLANES, rows, columns), lambda s, c: (s, 1 - c, 0, 0, 0)),
        compiler_params=params(10),
        cost_estimate=cost(7),
        name="diagonal_kernel",
    )(behind(start_late, fields), l_values, wave, edge)

    def passing(first, source, *others):
        return pl.pallas_call(
            functools.partial(pass_kernel, first),
            out_shape=[array(2, 2, HALF)] * 2,
            in_specs=[SMEM, VMEM],
            out_specs=[VMEM] * 2,
            compiler_params=params(8),
            cost_estimate=cost(1),
            name="pass_kernel",
        )(behind(passed, *others), source)

    up_one, down_three = passing(0, up_all, diag_step)
    down_one, up_three = passing(4, down_all, up_one)
    weights = behind(couple_weight, up_three)
    moved = [shift(v, by) for v, by in ((up_one, 1), (down_three, -3), (down_one, -1), (up_three, 3))]
    tables = [count, item, weights]
    totals = pl.pallas_call(
        own_kernel,
        out_shape=[array(HELD, 2, dtype=jnp.float32)] * PLANES,
        in_specs=[SMEM] * 3 + [HBM] + [VMEM] * (2 + PLANES),
        out_specs=[VMEM] * PLANES,
        scratch_shapes=[pltpu.VMEM((HELD, 2, PLANES, rows, columns), bf16), pltpu.SemaphoreType.DMA(())],
        compiler_params=params(8),
        cost_estimate=cost(9),
        name="own_kernel",
    )(*tables, wave, up_all, down_all, *fields)
    totals = pl.pallas_call(
        near_kernel,
        out_shape=[array(HELD, 2, dtype=jnp.float32)] * PLANES,
        in_specs=[SMEM] * 3 + [VMEM] * (2 + 2 * PLANES),
        out_specs=[VMEM] * PLANES,
        input_output_aliases={5 + PLANES + p: p for p in range(PLANES)},
        compiler_params=params(8),
        cost_estimate=cost(4),
        name="near_kernel",
    )(*tables, up_two, down_two, *fields, *totals)

    inputs = [*tables, *moved, *fields, *totals]
    coupling, *_ = pl.pallas_call(
        last_kernel,
        out_shape=[array(HELD, 2, PLANES)] + [array(HELD, 2, dtype=jnp.float32)] * PLANES,
        in_specs=[SMEM] * 3 + [VMEM] * (len(inputs) - 3),
        out_specs=[ANY] + [VMEM] * PLANES,
        scratch_shapes=[pltpu.VMEM((PLANES, HELD, 2, rows, columns), bf16), dma(PLANES * HELD)],
        input_output_aliases={len(inputs) - PLANES + p: 1 + p for p in range(PLANES)},
        compiler_params=params(16),
        cost_estimate=cost(3),
        name="last_kernel",
    )(*inputs)
    return diag_step, coupling


def solution(mesh):
    placed = (
        P("chan", None, None, "radial", None),
        P("chan", None),
        P(),
        P("chan", None),
        P("chan", None),
        P("chan", None),
        P(),
    )
    return jax.shard_map(
        shards,
        mesh=mesh,
        in_specs=placed,
        out_specs=(P("chan", None, None, "radial", None), P("chan", None, None, "radial", None)),
        check_vma=False,
    )
```

```python
import functools

import jax
import jax.numpy as jnp
from jax import lax
from jax.experimental import pallas as pl
from jax.experimental.pallas import tpu as pltpu
from jax.sharding import PartitionSpec as P

WSTART = 16
grid_step = 0.25
charge = 3.0
time_step = 0.02

HELD = 4
PARTS = 8
PLANES = 4
HALF = 2
EDGE = 16
ORDERS = 4
ENTRIES = HELD * PARTS
GROUPS = 5

PAIR_LOW = 1233667140
PAIR_HIGH = 1234062796


def two_of(mask):
    word = jnp.where(mask >= 8, PAIR_HIGH, PAIR_LOW)
    code = lax.shift_right_logical(word, 4 * (mask & 7)) & 15
    return code & 3, code >> 2


def needed(source_ref, slot_ref, device, offset, devices):
    reader = device + offset
    inside = (reader >= 0) & (reader < devices)
    row = jnp.clip(reader, 0, devices - 1) * HELD
    mask = jnp.int32(0)
    for i in range(HELD):
        for e in range(PARTS):
            slot = slot_ref[source_ref[e, row + i]]
            mask = mask | jnp.where(slot // HELD == device, jnp.int32(1) << (slot % HELD), 0)
    return two_of(jnp.where(inside, mask, 0))


def run(copies):
    for copy in copies:
        copy.start()
    for copy in copies:
        copy.wait()


def head_kernel(wave_ref, up_ref, down_ref, up_held, down_held, in_sem, out_sem):
    steps = []
    for s in range(HELD):
        for ref, held, start in ((up_ref, up_held, 0), (down_ref, down_held, HALF)):
            n = len(steps)
            steps.append((
                pltpu.make_async_copy(wave_ref.at[s, :, pl.ds(1 + start, HALF)], held.at[s], in_sem.at[n]),
                pltpu.make_async_copy(held.at[s], ref.at[s], out_sem.at[n]),
            ))
    for come, _ in steps:
        come.start()
    for come, go in steps:
        come.wait()
        go.start()
    for _, go in steps:
        go.wait()


def select_kernel(
    devices,
    edge_rows,
    me_ref,
    core_ref,
    sources,
    slots,
    wave_ref,
    up_ref,
    down_ref,
    edge_ref,
    source_ref,
    slot_ref,
    sem,
):
    rows = wave_ref.shape[3]
    at = pl.multiple_of((1 - core_ref[0]) * (rows - edge_rows), edge_rows)
    edge = pltpu.make_async_copy(
        wave_ref.at[:, :, pl.ds(1, PLANES), pl.ds(at, edge_rows)], edge_ref, sem.at[0]
    )
    edge.start()
    run([
        pltpu.make_async_copy(sources, source_ref, sem.at[1]),
        pltpu.make_async_copy(slots, slot_ref, sem.at[2]),
    ])
    me = me_ref[0]
    copies = []
    for ref, offset, start in ((up_ref, 1, HALF), (down_ref, -1, 0)):
        for i, pick in enumerate(needed(source_ref, slot_ref, me, offset, devices)):
            copies.append(
                pltpu.make_async_copy(
                    wave_ref.at[pick, :, pl.ds(1 + start, HALF)], ref.at[i], sem.at[3 + len(copies)]
                )
            )
    run(copies)
    edge.wait()


def item_kernel(
    devices, me_ref, sources, slots, pair_ref, order_ref, count_ref, item_ref, pass_ref, source_ref, slot_ref, sem
):
    run([
        pltpu.make_async_copy(sources, source_ref, sem.at[0]),
        pltpu.make_async_copy(slots, slot_ref, sem.at[1]),
    ])
    me = me_ref[0]

    def other(by):
        return lax.rem(me + by + devices, devices)

    for i, (by, offset) in enumerate(((-1, 2), (-1, -2), (1, -2), (1, 2))):
        pair = needed(source_ref, slot_ref, other(by), offset, devices)
        pass_ref[2 * i] = pair[0]
        pass_ref[2 * i + 1] = pair[1]
    firsts = [needed(source_ref, slot_ref, other(by), -by, devices)[0] for by in (-1, 1, -2, 2)]
    for g in range(GROUPS):
        count_ref[g] = jnp.int32(0)
    for s in range(HELD):
        for e in range(PARTS):
            slot = slot_ref[source_ref[e, me * HELD + s]]
            local, offset = slot % HELD, slot // HELD - me
            group, first = jnp.int32(0), jnp.int32(0)
            for g, by in enumerate((-1, 1, -2, 2)):
                group = jnp.where(offset == by, g + 1, group)
                first = jnp.where(offset == by, firsts[g], first)
            place = jnp.where(local == first, 0, 1)
            field = pair_ref[s, e] * ORDERS + order_ref[s, e]
            number = count_ref[group]
            item_ref[group, number] = (s * PARTS + e) + ENTRIES * (local + HELD * (place + 2 * field))
            count_ref[group] = number + 1


def pass_kernel(first, pass_ref, all_ref, one_ref, three_ref):
    for i in range(2):
        one_ref[i] = all_ref[pass_ref[first + i]]
        three_ref[i] = all_ref[pass_ref[first + 2 + i]]


def radius(shape, dim, start):
    return (start + lax.broadcasted_iota(jnp.int32, shape, dim) + 1).astype(jnp.float32) * grid_step


def field_kernel(row_ref, *out_refs):
    shape = out_refs[0].shape[1:]
    step = 16

    def tile(i, carry):
        at = pl.ds(pl.multiple_of(i * step, step), step)
        part = (step, shape[1])
        r_one = radius(part, 0, row_ref[0] + i * step)
        r_two = radius(part, 1, 0)

        def write(refs, pair, left, right):
            greater = jnp.maximum(left, right)
            value = 1.0 / greater
            ratio = jnp.minimum(left, right) / greater
            for order in range(ORDERS):
                for ref in refs:
                    ref[pair * ORDERS + order, at] = jnp.broadcast_to(value, part)
                value = value * ratio

        write(out_refs, 0, r_one, r_two)
        for p, ref in enumerate(out_refs):
            r_three = (WSTART + p + 1) * grid_step
            write([ref], 1, r_one, r_three)
            write([ref], 2, r_two, r_three)
        return carry

    lax.fori_loop(0, shape[0] // step, tile, 0)


def diagonal_kernel(row_ref, l_ref, wave_ref, edge_ref, out_ref):
    s, c = pl.program_id(0), pl.program_id(1)
    rows, columns = wave_ref.shape[3:]
    shape = (rows, columns)
    r_one = radius((rows, 1), 0, row_ref[0])
    r_two = radius((1, columns), 1, 0)

    def centrifugal(electron):
        number = l_ref[s, electron].astype(jnp.float32)
        return number * (number + 1.0)

    first = centrifugal(0) / (2.0 * r_one * r_one) - charge / r_one
    second = centrifugal(1) / (2.0 * r_two * r_two) - charge / r_two
    sign = jnp.where(c == 1, time_step, -time_step)
    lower_half = row_ref[0] == 0
    row = lax.broadcasted_iota(jnp.int32, shape, 0)
    column = lax.broadcasted_iota(jnp.int32, shape, 1)
    for p in range(PLANES):
        r_three = (WSTART + p + 1) * grid_step
        third = centrifugal(2) / (2.0 * r_three * r_three) - charge / r_three
        centre = wave_ref[0, 0, p + 1].astype(jnp.float32)
        edge = edge_ref[0, 0, p].astype(jnp.float32)
        above = jnp.where(lower_half, 0.0, edge[-1:])
        below = jnp.where(lower_half, edge[:1], 0.0)
        total = wave_ref[0, 0, p].astype(jnp.float32) + wave_ref[0, 0, p + 2].astype(jnp.float32)
        total = total + jnp.where(row == 0, above, pltpu.roll(centre, 1, 0))
        total = total + jnp.where(row == rows - 1, below, pltpu.roll(centre, rows - 1, 0))
        total = total + jnp.where(column == 0, 0.0, pltpu.roll(centre, 1, 1))
        total = total + jnp.where(column == columns - 1, 0.0, pltpu.roll(centre, columns - 1, 1))
        potential = first + (second + (third + 3.0 / (grid_step * grid_step)))
        energy = potential * centre - (0.5 / (grid_step * grid_step)) * total
        out_ref[0, 0, p] = (sign * energy).astype(out_ref.dtype)


def add_items(group, selected, p, count_ref, item_ref, weight_ref, field_ref, source_ref, total):
    rows = total.shape[2]
    step = 16

    def one(n, carry):
        code = item_ref[group, n]
        entry, rest = code % ENTRIES, code // ENTRIES
        s, e = entry // PARTS, entry % PARTS
        local, rest = rest % HELD, rest // HELD
        place, field = rest % 2, rest // 2
        place = place if selected else local
        weight = weight_ref[s, e]
        for i in range(rows // step):
            at = pl.ds(i * step, step)
            factor = weight * field_ref[field, at]
            for c in range(2):
                total[s, c, at] += factor * source_ref[place, c, p, at].astype(jnp.float32)
        return carry

    lax.fori_loop(0, count_ref[group], one, 0)


def own_kernel(count_ref, item_ref, weight_ref, wave_ref, up_all, down_all, *refs):
    fields, totals, own, sem = refs[:PLANES], refs[PLANES : 2 * PLANES], refs[-2], refs[-1]
    copy = pltpu.make_async_copy(wave_ref.at[:, :, pl.ds(1, PLANES)], own, sem)
    copy.start()
    for total in totals:
        total[...] = jnp.zeros_like(total)
    copy.wait()
    for p in range(PLANES):
        common = count_ref, item_ref, weight_ref, fields[p]
        add_items(0, False, p, *common, own, totals[p])
        group, ref = (1, up_all) if p < HALF else (2, down_all)
        add_items(group, False, p % HALF, *common, ref, totals[p])


def near_kernel(count_ref, item_ref, weight_ref, up_two, down_two, *refs):
    fields, totals = refs[:PLANES], refs[-PLANES:]
    for p in range(PLANES):
        group, ref = (2, down_two) if p < HALF else (1, up_two)
        add_items(group, True, p % HALF, count_ref, item_ref, weight_ref, fields[p], ref, totals[p])


def far_kernel(count_ref, item_ref, weight_ref, down_one, *refs):
    fields, totals = refs[:HALF], refs[-HALF:]
    for p in range(HALF):
        add_items(4, True, p, count_ref, item_ref, weight_ref, fields[p], down_one, totals[p])


def last_kernel(start, groups, count_ref, item_ref, weight_ref, *refs):
    fars, fields = refs[: len(groups)], refs[len(groups) : len(groups) + HALF]
    totals, out_ref, (staged, sem) = refs[-2 - HALF : -2], refs[-3 - HALF], refs[-2:]
    copies = []
    for p, total in enumerate(totals):
        for group, ref in zip(groups, fars):
            add_items(group, True, p, count_ref, item_ref, weight_ref, fields[p], ref, total)
        for s in range(HELD):
            staged[p, s, 0] = total[s, 1].astype(staged.dtype)
            staged[p, s, 1] = (-total[s, 0]).astype(staged.dtype)
            copies.append(
                pltpu.make_async_copy(staged.at[p, s], out_ref.at[s, :, start + p], sem.at[p * HELD + s])
            )
            copies[-1].start()
    for copy in copies:
        copy.wait()


ANY = pl.BlockSpec(memory_space=pl.ANY)
HBM = pl.BlockSpec(memory_space=pltpu.HBM)
VMEM = pl.BlockSpec(memory_space=pltpu.VMEM)
SMEM = pl.BlockSpec(memory_space=pltpu.SMEM)


def params(mib):
    return pltpu.CompilerParams(vmem_limit_bytes=mib << 20)


def cost(micros):
    return pl.CostEstimate(flops=0, bytes_accessed=micros * 3_000_000, transcendentals=0)


def behind(value, *others):
    return lax.optimization_barrier((value, others))[0]


def shards(wave, l_values, couple_source, couple_pair, couple_order, couple_weight, channel_slot):
    devices = lax.axis_size("chan")
    rows, columns = wave.shape[3:]
    me = lax.axis_index("chan").astype(jnp.int32).reshape(1)
    core = lax.axis_index("radial").astype(jnp.int32)
    row_start = (core * rows).reshape(1)
    bf16 = wave.dtype

    def array(*lead, dtype=bf16):
        return jax.ShapeDtypeStruct((*lead, rows, columns), dtype)

    sources = couple_source.T
    index_scratch = [pltpu.SMEM(sources.shape, jnp.int32), pltpu.SMEM(channel_slot.shape, jnp.int32)]

    def dma(number):
        return pltpu.SemaphoreType.DMA((number,))

    def shift(array, by):
        return lax.ppermute(array, "chan", [(i, (i + by) % devices) for i in range(devices)])

    def onward(array, source, by):
        pairs = []
        for i in range(devices):
            origin, target = (i + source) % devices, (i + by) % devices
            if abs(origin - target) == 2:
                pairs.append((i, target))
        return lax.ppermute(array, "chan", pairs)

    up_all, down_all = pl.pallas_call(
        head_kernel,
        out_shape=[array(HELD, 2, HALF)] * 2,
        in_specs=[HBM],
        out_specs=[ANY] * 2,
        scratch_shapes=[pltpu.VMEM((HELD, 2, HALF, rows, columns), bf16)] * 2 + [dma(2 * HELD)] * 2,
        compiler_params=params(60),
        cost_estimate=cost(2),
        name="head_kernel",
    )(wave)
    wave = behind(wave, up_all)
    up_all, down_all = shift(up_all, 1), shift(down_all, -1)
    up_two, down_two, edge = pl.pallas_call(
        functools.partial(select_kernel, devices, EDGE),
        out_shape=[*[array(2, 2, HALF)] * 2, jax.ShapeDtypeStruct((HELD, 2, PLANES, EDGE, columns), bf16)],
        in_specs=[SMEM, SMEM, HBM, HBM, HBM],
        out_specs=[VMEM] * 3,
        scratch_shapes=[*index_scratch, dma(7)],
        compiler_params=params(60),
        cost_estimate=cost(3),
        name="select_kernel",
    )(me, core.reshape(1), sources, channel_slot, wave)
    me_late, start_late = behind((me, row_start), up_two)
    up_two = shift(up_two, 1)
    down_two = shift(down_two, -1)
    edge = lax.ppermute(edge, "radial", [(0, 1), (1, 0)])

    count, item, passed = pl.pallas_call(
        functools.partial(item_kernel, devices),
        out_shape=(
            jax.ShapeDtypeStruct((GROUPS,), jnp.int32),
            jax.ShapeDtypeStruct((GROUPS, ENTRIES), jnp.int32),
            jax.ShapeDtypeStruct((8,), jnp.int32),
        ),
        in_specs=[SMEM, HBM, HBM, SMEM, SMEM],
        out_specs=(SMEM,) * 3,
        scratch_shapes=[*index_scratch, dma(2)],
        compiler_params=params(4),
        cost_estimate=cost(6),
        name="item_kernel",
    )(me_late, sources, channel_slot, couple_pair, couple_order)

    fields = pl.pallas_call(
        field_kernel,
        out_shape=[array(3 * ORDERS, dtype=jnp.float32)] * PLANES,
        in_specs=[SMEM],
        out_specs=[VMEM] * PLANES,
        compiler_params=params(16),
        cost_estimate=cost(2),
        name="field_kernel",
    )(behind(start_late, count))

    diag_step = pl.pallas_call(
        diagonal_kernel,
        grid=(HELD, 2),
        out_shape=array(HELD, 2, PLANES),
        in_specs=[
            SMEM,
            SMEM,
            pl.BlockSpec((1, 1, PLANES + 2, rows, columns), lambda s, c: (s, c, 0, 0, 0)),
            pl.BlockSpec((1, 1, PLANES, EDGE, columns), lambda s, c: (s, c, 0, 0, 0)),
        ],
        out_specs=pl.BlockSpec((1, 1, PLANES, rows, columns), lambda s, c: (s, 1 - c, 0, 0, 0)),
        compiler_params=params(10),
        cost_estimate=cost(7),
        name="diagonal_kernel",
    )(behind(start_late, fields), l_values, wave, edge)

    def passing(first, source, *others):
        return pl.pallas_call(
            functools.partial(pass_kernel, first),
            out_shape=[array(2, 2, HALF)] * 2,
            in_specs=[SMEM, VMEM],
            out_specs=[VMEM] * 2,
            compiler_params=params(8),
            cost_estimate=cost(1),
            name="pass_kernel",
        )(behind(passed, *others), source)

    up_one, down_three = passing(0, up_all, diag_step)
    down_one, up_three = passing(4, down_all, up_one)
    weights = behind(couple_weight, up_three)
    moved = [
        onward(v, *where)
        for v, where in ((up_one, (-1, 1)), (down_three, (-1, -3)), (down_one, (1, -1)), (up_three, (1, 3)))
    ]
    tables = [count, item, weights]
    totals = pl.pallas_call(
        own_kernel,
        out_shape=[array(HELD, 2, dtype=jnp.float32)] * PLANES,
        in_specs=[SMEM] * 3 + [HBM] + [VMEM] * (2 + PLANES),
        out_specs=[VMEM] * PLANES,
        scratch_shapes=[pltpu.VMEM((HELD, 2, PLANES, rows, columns), bf16), pltpu.SemaphoreType.DMA(())],
        compiler_params=params(8),
        cost_estimate=cost(9),
        name="own_kernel",
    )(*tables, wave, up_all, down_all, *fields)
    totals = pl.pallas_call(
        near_kernel,
        out_shape=[array(HELD, 2, dtype=jnp.float32)] * PLANES,
        in_specs=[SMEM] * 3 + [VMEM] * (2 + 2 * PLANES),
        out_specs=[VMEM] * PLANES,
        input_output_aliases={5 + PLANES + p: p for p in range(PLANES)},
        compiler_params=params(8),
        cost_estimate=cost(4),
        name="near_kernel",
    )(*tables, up_two, down_two, *fields, *totals)

    up_one, down_three, down_one, up_three = moved
    inputs = [*tables, down_one, *fields[HALF:], *totals[HALF:]]
    late = pl.pallas_call(
        far_kernel,
        out_shape=[array(HELD, 2, dtype=jnp.float32)] * HALF,
        in_specs=[SMEM] * 3 + [VMEM] * (len(inputs) - 3),
        out_specs=[VMEM] * HALF,
        input_output_aliases={len(inputs) - HALF + p: p for p in range(HALF)},
        compiler_params=params(8),
        cost_estimate=cost(1),
        name="far_kernel",
    )(*inputs)

    def last(start, groups, fars, totals, *coupling):
        inputs = [*tables, *fars, *fields[start : start + HALF], *totals, *coupling]
        first = len(inputs) - len(coupling) - HALF
        aliases = {first + p: 1 + p for p in range(HALF)} | {first + HALF: 0 for _ in coupling}
        return pl.pallas_call(
            functools.partial(last_kernel, start, groups),
            out_shape=[array(HELD, 2, PLANES)] + [array(HELD, 2, dtype=jnp.float32)] * HALF,
            in_specs=[SMEM] * 3 + [VMEM] * (first + HALF - 3) + [ANY] * len(coupling),
            out_specs=[ANY] + [VMEM] * HALF,
            scratch_shapes=[pltpu.VMEM((HALF, HELD, 2, rows, columns), bf16), dma(HALF * HELD)],
            input_output_aliases=aliases,
            compiler_params=params(12),
            cost_estimate=cost(2),
            name="last_kernel",
        )(*inputs)[0]

    soon = behind(totals[:HALF], late)
    coupling = last(0, (3, 4), (up_one, down_three), soon)
    coupling = last(HALF, (3,), (up_three,), late, coupling)
    return diag_step, coupling


def solution(mesh):
    placed = (
        P("chan", None, None, "radial", None),
        P("chan", None),
        P(),
        P("chan", None),
        P("chan", None),
        P("chan", None),
        P(),
    )
    return jax.shard_map(
        shards,
        mesh=mesh,
        in_specs=placed,
        out_specs=(P("chan", None, None, "radial", None), P("chan", None, None, "radial", None)),
        check_vma=False,
    )
```

```python
import functools

import jax
import jax.numpy as jnp
from jax import lax
from jax.experimental import pallas as pl
from jax.experimental.pallas import tpu as pltpu
from jax.sharding import PartitionSpec as P

WSTART = 16
grid_step = 0.25
charge = 3.0
time_step = 0.02

HELD = 4
PARTS = 8
PLANES = 4
HALF = 2
EDGE = 16
ORDERS = 4
ENTRIES = HELD * PARTS
GROUPS = 5

PAIR_LOW = 1233667140
PAIR_HIGH = 1234062796


def two_of(mask):
    word = jnp.where(mask >= 8, PAIR_HIGH, PAIR_LOW)
    code = lax.shift_right_logical(word, 4 * (mask & 7)) & 15
    return code & 3, code >> 2


def needed(source_ref, slot_ref, device, offset, devices):
    reader = device + offset
    inside = (reader >= 0) & (reader < devices)
    row = jnp.clip(reader, 0, devices - 1) * HELD
    mask = jnp.int32(0)
    for i in range(HELD):
        for e in range(PARTS):
            slot = slot_ref[source_ref[e, row + i]]
            mask = mask | jnp.where(slot // HELD == device, jnp.int32(1) << (slot % HELD), 0)
    return two_of(jnp.where(inside, mask, 0))


def run(copies):
    for copy in copies:
        copy.start()
    for copy in copies:
        copy.wait()


def head_kernel(wave_ref, up_ref, down_ref, up_held, down_held, in_sem, out_sem):
    steps = []
    for s in range(HELD):
        for ref, held, start in ((up_ref, up_held, 0), (down_ref, down_held, HALF)):
            n = len(steps)
            steps.append((
                pltpu.make_async_copy(wave_ref.at[s, :, pl.ds(1 + start, HALF)], held.at[s], in_sem.at[n]),
                pltpu.make_async_copy(held.at[s], ref.at[s], out_sem.at[n]),
            ))
    for come, _ in steps:
        come.start()
    for come, go in steps:
        come.wait()
        go.start()
    for _, go in steps:
        go.wait()


def select_kernel(
    devices,
    edge_rows,
    me_ref,
    core_ref,
    sources,
    slots,
    wave_ref,
    up_ref,
    down_ref,
    edge_ref,
    source_ref,
    slot_ref,
    sem,
):
    rows = wave_ref.shape[3]
    at = pl.multiple_of((1 - core_ref[0]) * (rows - edge_rows), edge_rows)
    edge = pltpu.make_async_copy(
        wave_ref.at[:, :, pl.ds(1, PLANES), pl.ds(at, edge_rows)], edge_ref, sem.at[0]
    )
    edge.start()
    run([
        pltpu.make_async_copy(sources, source_ref, sem.at[1]),
        pltpu.make_async_copy(slots, slot_ref, sem.at[2]),
    ])
    me = me_ref[0]
    copies = []
    for ref, offset, start in ((up_ref, 1, HALF), (down_ref, -1, 0)):
        for i, pick in enumerate(needed(source_ref, slot_ref, me, offset, devices)):
            copies.append(
                pltpu.make_async_copy(
                    wave_ref.at[pick, :, pl.ds(1 + start, HALF)], ref.at[i], sem.at[3 + len(copies)]
                )
            )
    run(copies)
    edge.wait()


def item_kernel(
    devices, me_ref, sources, slots, pair_ref, order_ref, count_ref, item_ref, pass_ref, source_ref, slot_ref, sem
):
    run([
        pltpu.make_async_copy(sources, source_ref, sem.at[0]),
        pltpu.make_async_copy(slots, slot_ref, sem.at[1]),
    ])
    me = me_ref[0]

    def other(by):
        return lax.rem(me + by + devices, devices)

    for i, (by, offset) in enumerate(((-1, 2), (-1, -2), (1, -2), (1, 2))):
        pair = needed(source_ref, slot_ref, other(by), offset, devices)
        pass_ref[2 * i] = pair[0]
        pass_ref[2 * i + 1] = pair[1]
    firsts = [needed(source_ref, slot_ref, other(by), -by, devices)[0] for by in (-1, 1, -2, 2)]
    for g in range(GROUPS):
        count_ref[g] = jnp.int32(0)
    for s in range(HELD):
        for e in range(PARTS):
            slot = slot_ref[source_ref[e, me * HELD + s]]
            local, offset = slot % HELD, slot // HELD - me
            group, first = jnp.int32(0), jnp.int32(0)
            for g, by in enumerate((-1, 1, -2, 2)):
                group = jnp.where(offset == by, g + 1, group)
                first = jnp.where(offset == by, firsts[g], first)
            place = jnp.where(local == first, 0, 1)
            field = pair_ref[s, e] * ORDERS + order_ref[s, e]
            number = count_ref[group]
            item_ref[group, number] = (s * PARTS + e) + ENTRIES * (local + HELD * (place + 2 * field))
            count_ref[group] = number + 1


def pass_kernel(first, pass_ref, all_ref, one_ref, three_ref):
    for i in range(2):
        one_ref[i] = all_ref[pass_ref[first + i]]
        three_ref[i] = all_ref[pass_ref[first + 2 + i]]


def radius(shape, dim, start):
    return (start + lax.broadcasted_iota(jnp.int32, shape, dim) + 1).astype(jnp.float32) * grid_step


def field_kernel(row_ref, *out_refs):
    shape = out_refs[0].shape[1:]
    step = 16

    def tile(i, carry):
        at = pl.ds(pl.multiple_of(i * step, step), step)
        part = (step, shape[1])
        r_one = radius(part, 0, row_ref[0] + i * step)
        r_two = radius(part, 1, 0)

        def write(refs, pair, left, right):
            greater = jnp.maximum(left, right)
            value = 1.0 / greater
            ratio = jnp.minimum(left, right) / greater
            for order in range(ORDERS):
                for ref in refs:
                    ref[pair * ORDERS + order, at] = jnp.broadcast_to(value, part)
                value = value * ratio

        write(out_refs, 0, r_one, r_two)
        for p, ref in enumerate(out_refs):
            r_three = (WSTART + p + 1) * grid_step
            write([ref], 1, r_one, r_three)
            write([ref], 2, r_two, r_three)
        return carry

    lax.fori_loop(0, shape[0] // step, tile, 0)


def diagonal_kernel(row_ref, l_ref, wave_ref, edge_ref, out_ref):
    s, c = pl.program_id(0), pl.program_id(1)
    rows, columns = wave_ref.shape[3:]
    shape = (rows, columns)
    r_one = radius((rows, 1), 0, row_ref[0])
    r_two = radius((1, columns), 1, 0)

    def centrifugal(electron):
        number = l_ref[s, electron].astype(jnp.float32)
        return number * (number + 1.0)

    first = centrifugal(0) / (2.0 * r_one * r_one) - charge / r_one
    second = centrifugal(1) / (2.0 * r_two * r_two) - charge / r_two
    sign = jnp.where(c == 1, time_step, -time_step)
    lower_half = row_ref[0] == 0
    row = lax.broadcasted_iota(jnp.int32, shape, 0)
    column = lax.broadcasted_iota(jnp.int32, shape, 1)
    for p in range(PLANES):
        r_three = (WSTART + p + 1) * grid_step
        third = centrifugal(2) / (2.0 * r_three * r_three) - charge / r_three
        centre = wave_ref[0, 0, p + 1].astype(jnp.float32)
        edge = edge_ref[0, 0, p].astype(jnp.float32)
        above = jnp.where(lower_half, 0.0, edge[-1:])
        below = jnp.where(lower_half, edge[:1], 0.0)
        total = wave_ref[0, 0, p].astype(jnp.float32) + wave_ref[0, 0, p + 2].astype(jnp.float32)
        total = total + jnp.where(row == 0, above, pltpu.roll(centre, 1, 0))
        total = total + jnp.where(row == rows - 1, below, pltpu.roll(centre, rows - 1, 0))
        total = total + jnp.where(column == 0, 0.0, pltpu.roll(centre, 1, 1))
        total = total + jnp.where(column == columns - 1, 0.0, pltpu.roll(centre, columns - 1, 1))
        potential = first + (second + (third + 3.0 / (grid_step * grid_step)))
        energy = potential * centre - (0.5 / (grid_step * grid_step)) * total
        out_ref[0, 0, p] = (sign * energy).astype(out_ref.dtype)


def add_items(group, selected, p, count_ref, item_ref, weight_ref, field_ref, source_ref, total):
    rows = total.shape[2]
    step = 16

    def one(n, carry):
        code = item_ref[group, n]
        entry, rest = code % ENTRIES, code // ENTRIES
        s, e = entry // PARTS, entry % PARTS
        local, rest = rest % HELD, rest // HELD
        place, field = rest % 2, rest // 2
        place = place if selected else local
        weight = weight_ref[s, e]
        for i in range(rows // step):
            at = pl.ds(i * step, step)
            factor = weight * field_ref[field, at]
            for c in range(2):
                total[s, c, at] += factor * source_ref[place, c, p, at].astype(jnp.float32)
        return carry

    lax.fori_loop(0, count_ref[group], one, 0)


def own_kernel(count_ref, item_ref, weight_ref, wave_ref, up_all, down_all, *refs):
    fields, totals, own, sem = refs[:PLANES], refs[PLANES : 2 * PLANES], refs[-2], refs[-1]
    copy = pltpu.make_async_copy(wave_ref.at[:, :, pl.ds(1, PLANES)], own, sem)
    copy.start()
    for total in totals:
        total[...] = jnp.zeros_like(total)
    copy.wait()
    for p in range(PLANES):
        common = count_ref, item_ref, weight_ref, fields[p]
        add_items(0, False, p, *common, own, totals[p])
        group, ref = (1, up_all) if p < HALF else (2, down_all)
        add_items(group, False, p % HALF, *common, ref, totals[p])


def near_kernel(count_ref, item_ref, weight_ref, up_two, down_two, *refs):
    fields, totals = refs[:PLANES], refs[-PLANES:]
    for p in range(PLANES):
        group, ref = (2, down_two) if p < HALF else (1, up_two)
        add_items(group, True, p % HALF, count_ref, item_ref, weight_ref, fields[p], ref, totals[p])


def far_kernel(count_ref, item_ref, weight_ref, up_one, down_one, *refs):
    fields, totals = refs[:PLANES], refs[-PLANES:]
    for p in range(PLANES):
        group, ref = (3, up_one) if p < HALF else (4, down_one)
        add_items(group, True, p % HALF, count_ref, item_ref, weight_ref, fields[p], ref, totals[p])


def last_kernel(start, groups, count_ref, item_ref, weight_ref, *refs):
    fars, fields = refs[: len(groups)], refs[len(groups) : len(groups) + HALF]
    totals, out_ref, (staged, sem) = refs[-2 - HALF : -2], refs[-3 - HALF], refs[-2:]
    copies = []
    for p, total in enumerate(totals):
        for group, ref in zip(groups, fars):
            add_items(group, True, p, count_ref, item_ref, weight_ref, fields[p], ref, total)
        for s in range(HELD):
            staged[p, s, 0] = total[s, 1].astype(staged.dtype)
            staged[p, s, 1] = (-total[s, 0]).astype(staged.dtype)
            copies.append(
                pltpu.make_async_copy(staged.at[p, s], out_ref.at[s, :, start + p], sem.at[p * HELD + s])
            )
            copies[-1].start()
    for copy in copies:
        copy.wait()


ANY = pl.BlockSpec(memory_space=pl.ANY)
HBM = pl.BlockSpec(memory_space=pltpu.HBM)
VMEM = pl.BlockSpec(memory_space=pltpu.VMEM)
SMEM = pl.BlockSpec(memory_space=pltpu.SMEM)


def params(mib):
    return pltpu.CompilerParams(vmem_limit_bytes=mib << 20)


def cost(micros):
    return pl.CostEstimate(flops=0, bytes_accessed=micros * 3_000_000, transcendentals=0)


def behind(value, *others):
    return lax.optimization_barrier((value, others))[0]


def shards(wave, l_values, couple_source, couple_pair, couple_order, couple_weight, channel_slot):
    devices = lax.axis_size("chan")
    rows, columns = wave.shape[3:]
    me = lax.axis_index("chan").astype(jnp.int32).reshape(1)
    core = lax.axis_index("radial").astype(jnp.int32)
    row_start = (core * rows).reshape(1)
    bf16 = wave.dtype

    def array(*lead, dtype=bf16):
        return jax.ShapeDtypeStruct((*lead, rows, columns), dtype)

    sources = couple_source.T
    index_scratch = [pltpu.SMEM(sources.shape, jnp.int32), pltpu.SMEM(channel_slot.shape, jnp.int32)]

    def dma(number):
        return pltpu.SemaphoreType.DMA((number,))

    def shift(array, by):
        return lax.ppermute(array, "chan", [(i, (i + by) % devices) for i in range(devices)])

    def onward(array, source, by):
        pairs = []
        for i in range(devices):
            origin, target = (i + source) % devices, (i + by) % devices
            if abs(origin - target) == 2:
                pairs.append((i, target))
        return lax.ppermute(array, "chan", pairs)

    up_all, down_all = pl.pallas_call(
        head_kernel,
        out_shape=[array(HELD, 2, HALF)] * 2,
        in_specs=[HBM],
        out_specs=[ANY] * 2,
        scratch_shapes=[pltpu.VMEM((HELD, 2, HALF, rows, columns), bf16)] * 2 + [dma(2 * HELD)] * 2,
        compiler_params=params(60),
        cost_estimate=cost(2),
        name="head_kernel",
    )(wave)
    wave = behind(wave, up_all)
    up_all, down_all = shift(up_all, 1), shift(down_all, -1)
    up_two, down_two, edge = pl.pallas_call(
        functools.partial(select_kernel, devices, EDGE),
        out_shape=[*[array(2, 2, HALF)] * 2, jax.ShapeDtypeStruct((HELD, 2, PLANES, EDGE, columns), bf16)],
        in_specs=[SMEM, SMEM, HBM, HBM, HBM],
        out_specs=[VMEM] * 3,
        scratch_shapes=[*index_scratch, dma(7)],
        compiler_params=params(60),
        cost_estimate=cost(3),
        name="select_kernel",
    )(me, core.reshape(1), sources, channel_slot, wave)
    me_late, start_late = behind((me, row_start), up_two)
    up_two = shift(up_two, 1)
    down_two = shift(down_two, -1)
    edge = lax.ppermute(edge, "radial", [(0, 1), (1, 0)])

    count, item, passed = pl.pallas_call(
        functools.partial(item_kernel, devices),
        out_shape=(
            jax.ShapeDtypeStruct((GROUPS,), jnp.int32),
            jax.ShapeDtypeStruct((GROUPS, ENTRIES), jnp.int32),
            jax.ShapeDtypeStruct((8,), jnp.int32),
        ),
        in_specs=[SMEM, HBM, HBM, SMEM, SMEM],
        out_specs=(SMEM,) * 3,
        scratch_shapes=[*index_scratch, dma(2)],
        compiler_params=params(4),
        cost_estimate=cost(6),
        name="item_kernel",
    )(me_late, sources, channel_slot, couple_pair, couple_order)

    fields = pl.pallas_call(
        field_kernel,
        out_shape=[array(3 * ORDERS, dtype=jnp.float32)] * PLANES,
        in_specs=[SMEM],
        out_specs=[VMEM] * PLANES,
        compiler_params=params(16),
        cost_estimate=cost(2),
        name="field_kernel",
    )(behind(start_late, count))

    diag_step = pl.pallas_call(
        diagonal_kernel,
        grid=(HELD, 2),
        out_shape=array(HELD, 2, PLANES),
        in_specs=[
            SMEM,
            SMEM,
            pl.BlockSpec((1, 1, PLANES + 2, rows, columns), lambda s, c: (s, c, 0, 0, 0)),
            pl.BlockSpec((1, 1, PLANES, EDGE, columns), lambda s, c: (s, c, 0, 0, 0)),
        ],
        out_specs=pl.BlockSpec((1, 1, PLANES, rows, columns), lambda s, c: (s, 1 - c, 0, 0, 0)),
        compiler_params=params(10),
        cost_estimate=cost(7),
        name="diagonal_kernel",
    )(behind(start_late, fields), l_values, wave, edge)

    def passing(first, source, *others):
        return pl.pallas_call(
            functools.partial(pass_kernel, first),
            out_shape=[array(2, 2, HALF)] * 2,
            in_specs=[SMEM, VMEM],
            out_specs=[VMEM] * 2,
            compiler_params=params(8),
            cost_estimate=cost(1),
            name="pass_kernel",
        )(behind(passed, *others), source)

    up_one, down_three = passing(0, up_all, diag_step)
    down_one, up_three = passing(4, down_all, up_one)
    weights = behind(couple_weight, up_three)
    down_three, up_three = behind(down_three, up_two), behind(up_three, down_two)
    moved = [
        onward(v, *where)
        for v, where in ((up_one, (-1, 1)), (down_three, (-1, -3)), (down_one, (1, -1)), (up_three, (1, 3)))
    ]
    tables = [count, item, weights]
    totals = pl.pallas_call(
        own_kernel,
        out_shape=[array(HELD, 2, dtype=jnp.float32)] * PLANES,
        in_specs=[SMEM] * 3 + [HBM] + [VMEM] * (2 + PLANES),
        out_specs=[VMEM] * PLANES,
        scratch_shapes=[pltpu.VMEM((HELD, 2, PLANES, rows, columns), bf16), pltpu.SemaphoreType.DMA(())],
        compiler_params=params(8),
        cost_estimate=cost(9),
        name="own_kernel",
    )(*tables, wave, up_all, down_all, *fields)
    totals = pl.pallas_call(
        near_kernel,
        out_shape=[array(HELD, 2, dtype=jnp.float32)] * PLANES,
        in_specs=[SMEM] * 3 + [VMEM] * (2 + 2 * PLANES),
        out_specs=[VMEM] * PLANES,
        input_output_aliases={5 + PLANES + p: p for p in range(PLANES)},
        compiler_params=params(8),
        cost_estimate=cost(4),
        name="near_kernel",
    )(*tables, up_two, down_two, *fields, *totals)

    up_one, down_three, down_one, up_three = moved
    inputs = [*tables, up_one, down_one, *fields, *totals]
    totals = pl.pallas_call(
        far_kernel,
        out_shape=[array(HELD, 2, dtype=jnp.float32)] * PLANES,
        in_specs=[SMEM] * 3 + [VMEM] * (len(inputs) - 3),
        out_specs=[VMEM] * PLANES,
        input_output_aliases={len(inputs) - PLANES + p: p for p in range(PLANES)},
        compiler_params=params(8),
        cost_estimate=cost(2),
        name="far_kernel",
    )(*inputs)

    def last(start, groups, fars, totals, *coupling):
        inputs = [*tables, *fars, *fields[start : start + HALF], *totals, *coupling]
        first = len(inputs) - len(coupling) - HALF
        aliases = {first + p: 1 + p for p in range(HALF)} | {first + HALF: 0 for _ in coupling}
        return pl.pallas_call(
            functools.partial(last_kernel, start, groups),
            out_shape=[array(HELD, 2, PLANES)] + [array(HELD, 2, dtype=jnp.float32)] * HALF,
            in_specs=[SMEM] * 3 + [VMEM] * (first + HALF - 3) + [ANY] * len(coupling),
            out_specs=[ANY] + [VMEM] * HALF,
            scratch_shapes=[pltpu.VMEM((HALF, HELD, 2, rows, columns), bf16), dma(HALF * HELD)],
            input_output_aliases=aliases,
            compiler_params=params(12),
            cost_estimate=cost(2),
            name="last_kernel",
        )(*inputs)[0]

    coupling = last(0, (4,), (down_three,), totals[:HALF])
    coupling = last(HALF, (3,), (up_three,), totals[HALF:], coupling)
    return diag_step, coupling


def solution(mesh):
    placed = (
        P("chan", None, None, "radial", None),
        P("chan", None),
        P(),
        P("chan", None),
        P("chan", None),
        P("chan", None),
        P(),
    )
    return jax.shard_map(
        shards,
        mesh=mesh,
        in_specs=placed,
        out_specs=(P("chan", None, None, "radial", None), P("chan", None, None, "radial", None)),
        check_vma=False,
    )
```

```python
import functools

import jax
import jax.numpy as jnp
from jax import lax
from jax.experimental import pallas as pl
from jax.experimental.pallas import tpu as pltpu
from jax.sharding import PartitionSpec as P

WSTART = 16
grid_step = 0.25
charge = 3.0
time_step = 0.02

HELD = 4
PARTS = 8
PLANES = 4
HALF = 2
EDGE = 16
ORDERS = 4
ENTRIES = HELD * PARTS
GROUPS = 5

PAIR_LOW = 1233667140
PAIR_HIGH = 1234062796


def two_of(mask):
    word = jnp.where(mask >= 8, PAIR_HIGH, PAIR_LOW)
    code = lax.shift_right_logical(word, 4 * (mask & 7)) & 15
    return code & 3, code >> 2


def needed(source_ref, slot_ref, device, offset, devices):
    reader = device + offset
    inside = (reader >= 0) & (reader < devices)
    row = jnp.clip(reader, 0, devices - 1) * HELD
    mask = jnp.int32(0)
    for i in range(HELD):
        for e in range(PARTS):
            slot = slot_ref[source_ref[e, row + i]]
            mask = mask | jnp.where(slot // HELD == device, jnp.int32(1) << (slot % HELD), 0)
    return two_of(jnp.where(inside, mask, 0))


def run(copies):
    for copy in copies:
        copy.start()
    for copy in copies:
        copy.wait()


def head_kernel(wave_ref, up_ref, down_ref, up_held, down_held, in_sem, out_sem):
    steps = []
    for s in range(HELD):
        for ref, held, start in ((up_ref, up_held, 0), (down_ref, down_held, HALF)):
            n = len(steps)
            steps.append((
                pltpu.make_async_copy(wave_ref.at[s, :, pl.ds(1 + start, HALF)], held.at[s], in_sem.at[n]),
                pltpu.make_async_copy(held.at[s], ref.at[s], out_sem.at[n]),
            ))
    for come, _ in steps:
        come.start()
    for come, go in steps:
        come.wait()
        go.start()
    for _, go in steps:
        go.wait()


def select_kernel(
    devices,
    edge_rows,
    me_ref,
    core_ref,
    sources,
    slots,
    wave_ref,
    up_ref,
    down_ref,
    edge_ref,
    source_ref,
    slot_ref,
    sem,
):
    rows = wave_ref.shape[3]
    at = pl.multiple_of((1 - core_ref[0]) * (rows - edge_rows), edge_rows)
    edge = pltpu.make_async_copy(
        wave_ref.at[:, :, pl.ds(1, PLANES), pl.ds(at, edge_rows)], edge_ref, sem.at[0]
    )
    edge.start()
    run([
        pltpu.make_async_copy(sources, source_ref, sem.at[1]),
        pltpu.make_async_copy(slots, slot_ref, sem.at[2]),
    ])
    me = me_ref[0]
    copies = []
    for ref, offset, start in ((up_ref, 1, HALF), (down_ref, -1, 0)):
        for i, pick in enumerate(needed(source_ref, slot_ref, me, offset, devices)):
            copies.append(
                pltpu.make_async_copy(
                    wave_ref.at[pick, :, pl.ds(1 + start, HALF)], ref.at[i], sem.at[3 + len(copies)]
                )
            )
    run(copies)
    edge.wait()


def item_kernel(
    devices, me_ref, sources, slots, pair_ref, order_ref, count_ref, item_ref, pass_ref, source_ref, slot_ref, sem
):
    run([
        pltpu.make_async_copy(sources, source_ref, sem.at[0]),
        pltpu.make_async_copy(slots, slot_ref, sem.at[1]),
    ])
    me = me_ref[0]

    def other(by):
        return lax.rem(me + by + devices, devices)

    for i, (by, offset) in enumerate(((-1, 2), (-1, -2), (1, -2), (1, 2))):
        pair = needed(source_ref, slot_ref, other(by), offset, devices)
        pass_ref[2 * i] = pair[0]
        pass_ref[2 * i + 1] = pair[1]
    firsts = [needed(source_ref, slot_ref, other(by), -by, devices)[0] for by in (-1, 1, -2, 2)]
    for g in range(GROUPS):
        count_ref[g, HELD] = jnp.int32(0)
    for s in range(HELD):
        for g in range(GROUPS):
            count_ref[g, s] = count_ref[g, HELD]
        for e in range(PARTS):
            slot = slot_ref[source_ref[e, me * HELD + s]]
            local, offset = slot % HELD, slot // HELD - me
            group, first = jnp.int32(0), jnp.int32(0)
            for g, by in enumerate((-1, 1, -2, 2)):
                group = jnp.where(offset == by, g + 1, group)
                first = jnp.where(offset == by, firsts[g], first)
            place = jnp.where(local == first, 0, 1)
            field = pair_ref[s, e] * ORDERS + order_ref[s, e]
            number = count_ref[group, HELD]
            item_ref[group, number] = (s * PARTS + e) + ENTRIES * (local + HELD * (place + 2 * field))
            count_ref[group, HELD] = number + 1


def pass_kernel(first, pass_ref, all_ref, one_ref, three_ref):
    for i in range(2):
        one_ref[i] = all_ref[pass_ref[first + i]]
        three_ref[i] = all_ref[pass_ref[first + 2 + i]]


def radius(shape, dim, start):
    return (start + lax.broadcasted_iota(jnp.int32, shape, dim) + 1).astype(jnp.float32) * grid_step


def field_kernel(row_ref, *out_refs):
    shape = out_refs[0].shape[1:]
    step = 16

    def tile(i, carry):
        at = pl.ds(pl.multiple_of(i * step, step), step)
        part = (step, shape[1])
        r_one = radius(part, 0, row_ref[0] + i * step)
        r_two = radius(part, 1, 0)

        def write(refs, pair, left, right):
            greater = jnp.maximum(left, right)
            value = 1.0 / greater
            ratio = jnp.minimum(left, right) / greater
            for order in range(ORDERS):
                for ref in refs:
                    ref[pair * ORDERS + order, at] = jnp.broadcast_to(value, part)
                value = value * ratio

        write(out_refs, 0, r_one, r_two)
        for p, ref in enumerate(out_refs):
            r_three = (WSTART + p + 1) * grid_step
            write([ref], 1, r_one, r_three)
            write([ref], 2, r_two, r_three)
        return carry

    lax.fori_loop(0, shape[0] // step, tile, 0)


def diagonal_kernel(row_ref, l_ref, wave_ref, edge_ref, out_ref):
    s, c = pl.program_id(0), pl.program_id(1)
    rows, columns = wave_ref.shape[3:]
    shape = (rows, columns)
    r_one = radius((rows, 1), 0, row_ref[0])
    r_two = radius((1, columns), 1, 0)

    def centrifugal(electron):
        number = l_ref[s, electron].astype(jnp.float32)
        return number * (number + 1.0)

    first = centrifugal(0) / (2.0 * r_one * r_one) - charge / r_one
    second = centrifugal(1) / (2.0 * r_two * r_two) - charge / r_two
    sign = jnp.where(c == 1, time_step, -time_step)
    lower_half = row_ref[0] == 0
    row = lax.broadcasted_iota(jnp.int32, shape, 0)
    column = lax.broadcasted_iota(jnp.int32, shape, 1)
    for p in range(PLANES):
        r_three = (WSTART + p + 1) * grid_step
        third = centrifugal(2) / (2.0 * r_three * r_three) - charge / r_three
        centre = wave_ref[0, 0, p + 1].astype(jnp.float32)
        edge = edge_ref[0, 0, p].astype(jnp.float32)
        above = jnp.where(lower_half, 0.0, edge[-1:])
        below = jnp.where(lower_half, edge[:1], 0.0)
        total = wave_ref[0, 0, p].astype(jnp.float32) + wave_ref[0, 0, p + 2].astype(jnp.float32)
        total = total + jnp.where(row == 0, above, pltpu.roll(centre, 1, 0))
        total = total + jnp.where(row == rows - 1, below, pltpu.roll(centre, rows - 1, 0))
        total = total + jnp.where(column == 0, 0.0, pltpu.roll(centre, 1, 1))
        total = total + jnp.where(column == columns - 1, 0.0, pltpu.roll(centre, columns - 1, 1))
        potential = first + (second + (third + 3.0 / (grid_step * grid_step)))
        energy = potential * centre - (0.5 / (grid_step * grid_step)) * total
        out_ref[0, 0, p] = (sign * energy).astype(out_ref.dtype)


def add_items(group, selected, p, count_ref, item_ref, weight_ref, field_ref, source_ref, total, channel=None):
    rows = total.shape[2]
    step = 16

    def one(n, carry):
        code = item_ref[group, n]
        entry, rest = code % ENTRIES, code // ENTRIES
        s, e = entry // PARTS, entry % PARTS
        local, rest = rest % HELD, rest // HELD
        place, field = rest % 2, rest // 2
        place = place if selected else local
        weight = weight_ref[s, e]
        for i in range(rows // step):
            at = pl.ds(i * step, step)
            factor = weight * field_ref[field, at]
            for c in range(2):
                total[s, c, at] += factor * source_ref[place, c, p, at].astype(jnp.float32)
        return carry

    begin = 0 if channel is None else count_ref[group, channel]
    end = count_ref[group, HELD if channel is None else channel + 1]
    lax.fori_loop(begin, end, one, 0)


def own_kernel(count_ref, item_ref, weight_ref, wave_ref, up_all, down_all, *refs):
    fields, totals, own, sem = refs[:PLANES], refs[PLANES : 2 * PLANES], refs[-2], refs[-1]
    copy = pltpu.make_async_copy(wave_ref.at[:, :, pl.ds(1, PLANES)], own, sem)
    copy.start()
    for total in totals:
        total[...] = jnp.zeros_like(total)
    copy.wait()
    for p in range(PLANES):
        common = count_ref, item_ref, weight_ref, fields[p]
        add_items(0, False, p, *common, own, totals[p])
        group, ref = (1, up_all) if p < HALF else (2, down_all)
        add_items(group, False, p % HALF, *common, ref, totals[p])


def near_kernel(count_ref, item_ref, weight_ref, up_two, down_two, *refs):
    fields, totals = refs[:PLANES], refs[-PLANES:]
    for p in range(PLANES):
        group, ref = (2, down_two) if p < HALF else (1, up_two)
        add_items(group, True, p % HALF, count_ref, item_ref, weight_ref, fields[p], ref, totals[p])


def far_kernel(count_ref, item_ref, weight_ref, up_one, down_one, *refs):
    fields, totals = refs[:PLANES], refs[-PLANES:]
    for p in range(PLANES):
        group, ref = (3, up_one) if p < HALF else (4, down_one)
        add_items(group, True, p % HALF, count_ref, item_ref, weight_ref, fields[p], ref, totals[p])


def last_kernel(start, groups, count_ref, item_ref, weight_ref, *refs):
    fars, fields = refs[: len(groups)], refs[len(groups) : len(groups) + HALF]
    totals, out_ref, (staged, sem) = refs[-2 - HALF : -2], refs[-3 - HALF], refs[-2:]
    copies = []
    for p, total in enumerate(totals):
        for s in range(HELD):
            for group, ref in zip(groups, fars):
                add_items(group, True, p, count_ref, item_ref, weight_ref, fields[p], ref, total, s)
            staged[p, s, 0] = total[s, 1].astype(staged.dtype)
            staged[p, s, 1] = (-total[s, 0]).astype(staged.dtype)
            copies.append(
                pltpu.make_async_copy(staged.at[p, s], out_ref.at[s, :, start + p], sem.at[p * HELD + s])
            )
            copies[-1].start()
    for copy in copies:
        copy.wait()


ANY = pl.BlockSpec(memory_space=pl.ANY)
HBM = pl.BlockSpec(memory_space=pltpu.HBM)
VMEM = pl.BlockSpec(memory_space=pltpu.VMEM)
SMEM = pl.BlockSpec(memory_space=pltpu.SMEM)


def params(mib):
    return pltpu.CompilerParams(vmem_limit_bytes=mib << 20)


def cost(micros):
    return pl.CostEstimate(flops=0, bytes_accessed=micros * 3_000_000, transcendentals=0)


def behind(value, *others):
    return lax.optimization_barrier((value, others))[0]


def shards(wave, l_values, couple_source, couple_pair, couple_order, couple_weight, channel_slot):
    devices = lax.axis_size("chan")
    rows, columns = wave.shape[3:]
    me = lax.axis_index("chan").astype(jnp.int32).reshape(1)
    core = lax.axis_index("radial").astype(jnp.int32)
    row_start = (core * rows).reshape(1)
    bf16 = wave.dtype

    def array(*lead, dtype=bf16):
        return jax.ShapeDtypeStruct((*lead, rows, columns), dtype)

    sources = couple_source.T
    index_scratch = [pltpu.SMEM(sources.shape, jnp.int32), pltpu.SMEM(channel_slot.shape, jnp.int32)]

    def dma(number):
        return pltpu.SemaphoreType.DMA((number,))

    def shift(array, by):
        return lax.ppermute(array, "chan", [(i, (i + by) % devices) for i in range(devices)])

    def onward(array, source, by):
        pairs = []
        for i in range(devices):
            origin, target = (i + source) % devices, (i + by) % devices
            if abs(origin - target) == 2:
                pairs.append((i, target))
        return lax.ppermute(array, "chan", pairs)

    up_all, down_all = pl.pallas_call(
        head_kernel,
        out_shape=[array(HELD, 2, HALF)] * 2,
        in_specs=[HBM],
        out_specs=[ANY] * 2,
        scratch_shapes=[pltpu.VMEM((HELD, 2, HALF, rows, columns), bf16)] * 2 + [dma(2 * HELD)] * 2,
        compiler_params=params(60),
        cost_estimate=cost(2),
        name="head_kernel",
    )(wave)
    wave = behind(wave, up_all)
    up_all, down_all = shift(up_all, 1), shift(down_all, -1)
    up_two, down_two, edge = pl.pallas_call(
        functools.partial(select_kernel, devices, EDGE),
        out_shape=[*[array(2, 2, HALF)] * 2, jax.ShapeDtypeStruct((HELD, 2, PLANES, EDGE, columns), bf16)],
        in_specs=[SMEM, SMEM, HBM, HBM, HBM],
        out_specs=[VMEM] * 3,
        scratch_shapes=[*index_scratch, dma(7)],
        compiler_params=params(60),
        cost_estimate=cost(3),
        name="select_kernel",
    )(me, core.reshape(1), sources, channel_slot, wave)
    me_late, start_late = behind((me, row_start), up_two)
    up_two = shift(up_two, 1)
    down_two = shift(down_two, -1)
    edge = lax.ppermute(edge, "radial", [(0, 1), (1, 0)])

    count, item, passed = pl.pallas_call(
        functools.partial(item_kernel, devices),
        out_shape=(
            jax.ShapeDtypeStruct((GROUPS, HELD + 1), jnp.int32),
            jax.ShapeDtypeStruct((GROUPS, ENTRIES), jnp.int32),
            jax.ShapeDtypeStruct((8,), jnp.int32),
        ),
        in_specs=[SMEM, HBM, HBM, SMEM, SMEM],
        out_specs=(SMEM,) * 3,
        scratch_shapes=[*index_scratch, dma(2)],
        compiler_params=params(4),
        cost_estimate=cost(6),
        name="item_kernel",
    )(me_late, sources, channel_slot, couple_pair, couple_order)

    fields = pl.pallas_call(
        field_kernel,
        out_shape=[array(3 * ORDERS, dtype=jnp.float32)] * PLANES,
        in_specs=[SMEM],
        out_specs=[VMEM] * PLANES,
        compiler_params=params(16),
        cost_estimate=cost(2),
        name="field_kernel",
    )(behind(start_late, count))

    diag_step = pl.pallas_call(
        diagonal_kernel,
        grid=(HELD, 2),
        out_shape=array(HELD, 2, PLANES),
        in_specs=[
            SMEM,
            SMEM,
            pl.BlockSpec((1, 1, PLANES + 2, rows, columns), lambda s, c: (s, c, 0, 0, 0)),
            pl.BlockSpec((1, 1, PLANES, EDGE, columns), lambda s, c: (s, c, 0, 0, 0)),
        ],
        out_specs=pl.BlockSpec((1, 1, PLANES, rows, columns), lambda s, c: (s, 1 - c, 0, 0, 0)),
        compiler_params=params(10),
        cost_estimate=cost(7),
        name="diagonal_kernel",
    )(behind(start_late, fields), l_values, wave, edge)

    def passing(first, source, *others):
        return pl.pallas_call(
            functools.partial(pass_kernel, first),
            out_shape=[array(2, 2, HALF)] * 2,
            in_specs=[SMEM, VMEM],
            out_specs=[VMEM] * 2,
            compiler_params=params(8),
            cost_estimate=cost(1),
            name="pass_kernel",
        )(behind(passed, *others), source)

    up_one, down_three = passing(0, up_all, diag_step)
    down_one, up_three = passing(4, down_all, up_one)
    weights = behind(couple_weight, up_three)
    down_three, up_three = behind(down_three, up_two), behind(up_three, down_two)
    moved = [
        onward(v, *where)
        for v, where in ((up_one, (-1, 1)), (down_three, (-1, -3)), (down_one, (1, -1)), (up_three, (1, 3)))
    ]
    tables = [count, item, weights]
    totals = pl.pallas_call(
        own_kernel,
        out_shape=[array(HELD, 2, dtype=jnp.float32)] * PLANES,
        in_specs=[SMEM] * 3 + [HBM] + [VMEM] * (2 + PLANES),
        out_specs=[VMEM] * PLANES,
        scratch_shapes=[pltpu.VMEM((HELD, 2, PLANES, rows, columns), bf16), pltpu.SemaphoreType.DMA(())],
        compiler_params=params(8),
        cost_estimate=cost(9),
        name="own_kernel",
    )(*tables, wave, up_all, down_all, *fields)
    totals = pl.pallas_call(
        near_kernel,
        out_shape=[array(HELD, 2, dtype=jnp.float32)] * PLANES,
        in_specs=[SMEM] * 3 + [VMEM] * (2 + 2 * PLANES),
        out_specs=[VMEM] * PLANES,
        input_output_aliases={5 + PLANES + p: p for p in range(PLANES)},
        compiler_params=params(8),
        cost_estimate=cost(4),
        name="near_kernel",
    )(*tables, up_two, down_two, *fields, *totals)

    up_one, down_three, down_one, up_three = moved
    inputs = [*tables, up_one, down_one, *fields, *totals]
    totals = pl.pallas_call(
        far_kernel,
        out_shape=[array(HELD, 2, dtype=jnp.float32)] * PLANES,
        in_specs=[SMEM] * 3 + [VMEM] * (len(inputs) - 3),
        out_specs=[VMEM] * PLANES,
        input_output_aliases={len(inputs) - PLANES + p: p for p in range(PLANES)},
        compiler_params=params(8),
        cost_estimate=cost(2),
        name="far_kernel",
    )(*inputs)

    def last(start, groups, fars, totals, *coupling):
        inputs = [*tables, *fars, *fields[start : start + HALF], *totals, *coupling]
        first = len(inputs) - len(coupling) - HALF
        aliases = {first + p: 1 + p for p in range(HALF)} | {first + HALF: 0 for _ in coupling}
        return pl.pallas_call(
            functools.partial(last_kernel, start, groups),
            out_shape=[array(HELD, 2, PLANES)] + [array(HELD, 2, dtype=jnp.float32)] * HALF,
            in_specs=[SMEM] * 3 + [VMEM] * (first + HALF - 3) + [ANY] * len(coupling),
            out_specs=[ANY] + [VMEM] * HALF,
            scratch_shapes=[pltpu.VMEM((HALF, HELD, 2, rows, columns), bf16), dma(HALF * HELD)],
            input_output_aliases=aliases,
            compiler_params=params(12),
            cost_estimate=cost(2),
            name="last_kernel",
        )(*inputs)[0]

    coupling = last(0, (4,), (down_three,), totals[:HALF])
    coupling = last(HALF, (3,), (up_three,), totals[HALF:], coupling)
    return diag_step, coupling


def solution(mesh):
    placed = (
        P("chan", None, None, "radial", None),
        P("chan", None),
        P(),
        P("chan", None),
        P("chan", None),
        P("chan", None),
        P(),
    )
    return jax.shard_map(
        shards,
        mesh=mesh,
        in_specs=placed,
        out_specs=(P("chan", None, None, "radial", None), P("chan", None, None, "radial", None)),
        check_vma=False,
    )
```
